32 devices in a mesh: groups: 2 (over x), tensor: 16 (over z, y, core).
Axes of the slice: x: 2, y: 2, z: 4, core: 2. Of those that a mesh axis runs over, the one named last changes fastest.
Arguments:
- hidden: bfloat16 [4, 256, 16384], P(None, 'groups', 'tensor'), parts along dimension 1, may hold values from -6 to 6
- down_matrix: bfloat16 [16384, 8192], P('tensor'), may hold values from -0.046875 to 0.046875
- first_factor_table: bfloat16 [256, 16, 16384], P(('groups', 'tensor')), parts along dimension 0, may hold values from -0.046875 to 0.046875
- second_factor_table: bfloat16 [256, 16, 8192], P(('groups', 'tensor')), parts along dimension 0, may hold values from -1.5 to 1.5
- adapter_storage_index: int32 [256], P('groups'), parts along dimension 0, may hold values from 0 to 127, as said below
- request_adapter: int32 [256], P('groups'), parts along dimension 0, may hold values from 0 to 127, as said below
Outputs:
- mixed: bfloat16 [4, 256, 8192], P(None, 'groups', 'tensor'), parts along dimension 1
The draws below stay inside these ranges and needn't reach their ends.
There are 2 independent parts, one for each index of `groups`. The reference program is written for one: setup_inputs(seed, part) draws one part's arguments, and reference() takes and returns one part's arrays. A program takes and returns all parts, laid end to end along the dimension named above; an argument that names none is the same for every part. Nothing has to cross between parts.
Inputs may be any that keep to these rules, and one draw needn't show every extreme that they name: `adapter_storage_index`: a permutation: each slot holds one adapter. `request_adapter`: at most 32 requests name adapters whose slots lie in one aligned block of 8 slots, and some block has exactly 32.
All inputs are finite; a program needn't handle non-finite values.
Results may differ from the reference program's by a relative error of at most 0.0041.
Values may be sent and summed in bfloat16 or wider, within the bound.
No kernel may reach another device: no remote copies, remote signals or barrier semaphores. Data moves between devices by JAX's collectives and lax.ppermute only.
A program may use at most 192 MiB of HBM per device.

```python
import jax
import jax.numpy as jnp
from jax import lax

MODEL_WIDTH = 8192
HIDDEN_UNITS = 16384
ADAPTER_RANK = 16
ADP_DEV = 8
STEPS = 4
ROWS = 128
ADAPTER_TOTAL = 128
CAP = 32


def storage_slots(key):
    return jax.random.permutation(jax.random.fold_in(key, 11), ADAPTER_TOTAL).astype(jnp.int32)


def draw_adapter_storage_index(key, part):
    return storage_slots(key)


def draw_request_adapter(key, part):
    slots = storage_slots(key)
    key = jax.random.fold_in(key, 5)
    devices = ADAPTER_TOTAL // ADP_DEV
    order = jax.random.permutation(jax.random.fold_in(key, 1), devices).astype(jnp.int32)
    places = jnp.arange(ROWS, dtype=jnp.int32)
    others = order[1 + (places - CAP) % (devices - 1)]
    owner = jnp.where(places < CAP, order[0], others)
    first_product = jax.random.randint(jax.random.fold_in(key, 2), (ROWS,), 0, ADP_DEV)
    second_product = jax.random.randint(jax.random.fold_in(key, 3), (ROWS,), 0, ADP_DEV)
    local = jnp.minimum(first_product, second_product).astype(jnp.int32)
    wanted = owner * ADP_DEV + local
    inverse = jnp.argsort(slots).astype(jnp.int32)
    ordered = inverse[wanted]
    shuffle = jax.random.permutation(jax.random.fold_in(key, 4), ROWS)
    return ordered[shuffle].astype(jnp.int32)


def block_levels(stream_key, dims, cuts, least, largest):
    def one(axis_at, parts):
        heights = jax.random.uniform(jax.random.fold_in(jax.random.fold_in(stream_key, 6), axis_at), (parts,), jnp.float32, least / len(cuts), largest / len(cuts))
        return jnp.repeat(jnp.exp(heights), dims[axis_at] // parts).reshape((-1,) + (1,) * (len(dims) - axis_at - 1))

    loudness = one(*cuts[0])
    for cut in cuts[1:]:
        loudness = loudness * one(*cut)
    return loudness


def normal_values(own_key, extent, scale, most, split=(), held_as=jnp.bfloat16):
    level = block_levels(own_key, extent, split, -0.22, 0.18) if split else 1.0
    values = jax.random.normal(own_key, extent, jnp.float32) * scale * level
    return jnp.minimum(jnp.maximum(values, -most), most).astype(held_as)


def setup_inputs(seed: int = 0, part: int = 0) -> dict:
    streams_of = jax.random.split(jax.random.key(seed), 7)
    part_splits = jax.random.split(jax.random.fold_in(streams_of[6], part), 7)
    return {
        "hidden": normal_values(part_splits[0], (STEPS, ROWS, HIDDEN_UNITS), 1.0, 6.0, ((2, 16),)),
        "down_matrix": normal_values(streams_of[1], (HIDDEN_UNITS, MODEL_WIDTH), HIDDEN_UNITS ** -0.5, 0.046875, ((0, 16),)),
        "first_factor_table": normal_values(part_splits[2], (ADAPTER_TOTAL, ADAPTER_RANK, HIDDEN_UNITS), HIDDEN_UNITS ** -0.5, 0.046875, ((0, 16),)),
        "second_factor_table": normal_values(part_splits[3], (ADAPTER_TOTAL, ADAPTER_RANK, MODEL_WIDTH), ADAPTER_RANK ** -0.5, 1.5, ((0, 16),)),
        "adapter_storage_index": draw_adapter_storage_index(jax.random.fold_in(jax.random.fold_in(streams_of[6], part), 71), part),
        "request_adapter": draw_request_adapter(jax.random.fold_in(jax.random.fold_in(streams_of[6], part), 71), part),
    }


def reference(hidden, down_matrix, first_factor_table, second_factor_table, adapter_storage_index, request_adapter):
    storage_index = adapter_storage_index[request_adapter]
    base = jnp.dot(hidden.reshape(STEPS * ROWS, HIDDEN_UNITS), down_matrix, preferred_element_type=jnp.float32)
    base = base.reshape(STEPS, ROWS, MODEL_WIDTH)
    first_product = first_factor_table[storage_index].astype(jnp.float32)
    low = jnp.einsum("srf,rkf->srk", hidden.astype(jnp.float32), first_product, precision=lax.Precision.HIGHEST)
    low = low.astype(jnp.bfloat16)
    second_product = second_factor_table[storage_index].astype(jnp.float32)
    extra = jnp.einsum("srk,rkd->srd", low.astype(jnp.float32), second_product, precision=lax.Precision.HIGHEST)
    return (base + extra).astype(jnp.bfloat16)
```

```python
import jax
import jax.numpy as jnp
from jax import lax
from jax.experimental import pallas as pl
from jax.experimental.pallas import tpu as pltpu
from jax.sharding import PartitionSpec as P

PLANE = 4
F32 = jnp.float32
BF16 = jnp.bfloat16
VMEM_BYTES = 48 * 1024 * 1024
LOW_CHUNKS = ((0, 2), (2, 4))
SUM_CHUNKS = ((0, 1), (1, 2), (2, 3), (3, 4))


def params():
    return pltpu.CompilerParams(vmem_limit_bytes=VMEM_BYTES)


def pack_factors(place, table, planes, width):
    rows = table.shape[0]

    def body(place_ref, *refs):
        for i in range(PLANE - 1):
            refs[PLANE - 1 + i][0] = refs[i][...]

    def columns(other):
        return lambda i, place_ref: (0, i * PLANE + (place_ref[1] ^ other))

    return pl.pallas_call(
        body,
        grid_spec=pltpu.PrefetchScalarGridSpec(
            num_scalar_prefetch=1,
            grid=(planes,),
            in_specs=[pl.BlockSpec((rows, width), columns(o)) for o in range(1, PLANE)],
            out_specs=[pl.BlockSpec((1, rows, width), lambda i, p: (i, 0, 0))] * (PLANE - 1),
        ),
        out_shape=[jax.ShapeDtypeStruct((planes, rows, width), BF16)] * (PLANE - 1),
        compiler_params=params(),
        name="pack_factors",
    )(place, table, table, table)


def base_blocks(place, hidden, down, planes, width):
    steps, rows, units = hidden.shape

    def body(place_ref, hidden_ref, d0, d1, d2, d3, send_ref, keep_ref):
        flat = hidden_ref[...].reshape(steps * rows, units)
        for i, ref in enumerate((d0, d1, d2, d3)):
            value = jnp.dot(flat, ref[...], preferred_element_type=F32).reshape(steps, rows, width)
            if i & 1:
                send_ref[i >> 1, 0] = value.astype(BF16)
            else:
                keep_ref[i >> 1, 0] = value

    def columns(other):
        return lambda i, p: (0, (p[0] ^ i) * PLANE + (p[1] ^ other))

    shape = (2, planes, steps, rows, width)
    return pl.pallas_call(
        body,
        grid_spec=pltpu.PrefetchScalarGridSpec(
            num_scalar_prefetch=1,
            grid=(planes,),
            in_specs=[pl.BlockSpec((steps, rows, units), lambda i, p: (0, 0, 0))]
            + [pl.BlockSpec((units, width), columns(o)) for o in range(PLANE)],
            out_specs=[pl.BlockSpec((2, 1, steps, rows, width), lambda i, p: (0, i, 0, 0, 0))] * 2,
        ),
        out_shape=[jax.ShapeDtypeStruct(shape, BF16), jax.ShapeDtypeStruct(shape, F32)],
        compiler_params=params(),
        name="base_blocks",
    )(place, hidden, down, down, down, down)


def low_part(place, order, slots, table, received, gathered, per_shard, rank):
    planes = len(gathered)
    rows, width = table.shape[0], gathered[0].shape[-1]
    steps, requests = gathered[0].shape[:2]
    lanes = steps * requests

    def body(place_ref, order_ref, slots_ref, a0, a1, a2, a3, *refs):
        hidden_refs, (out_ref, held, total) = refs[:planes], refs[planes:]
        j = pl.program_id(0)
        for i, ref in enumerate(hidden_refs):

            @pl.when(j == i)
            def _():
                held[...] = ref[...].reshape(lanes, width)

        @pl.when(j == 0)
        def _():
            total[...] = jnp.zeros_like(total)

        block = held[...]
        for i, ref in enumerate((a0, a1, a2, a3)):
            factors = ref[...] if i == 0 else ref[0]
            total[i] += lax.dot_general(
                factors, block, (((1,), (1,)), ((), ())), preferred_element_type=F32
            )

        @pl.when(j == planes - 1)
        def _():
            low = jnp.zeros((rank, lanes), F32)
            wanted = slots_ref[...]
            for i in range(PLANE):
                first = (place_ref[0] * PLANE + (place_ref[1] ^ i)) * per_shard
                for a in range(per_shard):
                    part = total[i, a * rank : (a + 1) * rank, :]
                    low += jnp.where(wanted == first + a, part, 0.0)
            out_ref[...] = low

    return pl.pallas_call(
        body,
        grid_spec=pltpu.PrefetchScalarGridSpec(
            num_scalar_prefetch=2,
            grid=(planes,),
            in_specs=[
                pl.BlockSpec((1, lanes), lambda j, p, o: (0, 0)),
                pl.BlockSpec((rows, width), lambda j, p, o: (0, o[j] * PLANE + p[1])),
            ]
            + [pl.BlockSpec((1, rows, width), lambda j, p, o: (o[j], 0, 0))] * (PLANE - 1)
            + [pl.BlockSpec((steps, requests, width), lambda j, p, o: (0, 0, 0))] * planes,
            out_specs=pl.BlockSpec((rank, lanes), lambda j, p, o: (0, 0)),
            scratch_shapes=[pltpu.VMEM((lanes, width), BF16), pltpu.VMEM((PLANE, rows, lanes), F32)],
        ),
        out_shape=jax.ShapeDtypeStruct((rank, lanes), F32),
        compiler_params=params(),
        name="low_part",
    )(place, order, slots, table, *received, *gathered)


def add_extra(place, low, slots, table, send, keep, chunk, per_shard, rank):
    _, planes, _, requests, width = send.shape
    first_step, last_step = chunk
    steps = last_step - first_step
    lanes = steps * requests
    rows = table.shape[0]

    def body(place_ref, low_ref, slots_ref, b0, b1, b2, b3, s_ref, k_ref, so_ref, ko_ref, spread):
        @pl.when(pl.program_id(0) == 0)
        def _():
            rounded = low_ref[...].astype(BF16).astype(F32)
            wanted = slots_ref[...]
            first = (place_ref[0] * PLANE + place_ref[1]) * per_shard
            parts = [jnp.where(wanted == first + a, rounded, 0.0) for a in range(per_shard)]
            spread[...] = jnp.concatenate(parts, axis=0).T.astype(BF16)

        rows_of = spread[...]
        for i, ref in enumerate((b0, b1, b2, b3)):
            extra = jnp.dot(rows_of, ref[...], preferred_element_type=F32)
            if i & 1:
                value = s_ref[i >> 1, 0].reshape(lanes, width).astype(F32) + extra
                so_ref[i >> 1, 0] = value.astype(BF16)
            else:
                ko_ref[i >> 1, 0] = k_ref[i >> 1, 0].reshape(lanes, width) + extra

    def columns(other):
        return lambda i, p: (0, (p[0] ^ i) * PLANE + (p[1] ^ other))

    base = pl.BlockSpec((2, 1, steps, requests, width), lambda i, p: (0, i, first_step // steps, 0, 0))
    shape = (2, planes, lanes, width)
    return pl.pallas_call(
        body,
        grid_spec=pltpu.PrefetchScalarGridSpec(
            num_scalar_prefetch=1,
            grid=(planes,),
            in_specs=[
                pl.BlockSpec((rank, lanes), lambda i, p: (0, 0)),
                pl.BlockSpec((1, lanes), lambda i, p: (0, 0)),
            ]
            + [pl.BlockSpec((rows, width), columns(o)) for o in range(PLANE)]
            + [base, base],
            out_specs=[pl.BlockSpec((2, 1, lanes, width), lambda i, p: (0, i, 0, 0))] * 2,
            scratch_shapes=[pltpu.VMEM((lanes, rows), BF16)],
        ),
        out_shape=[jax.ShapeDtypeStruct(shape, BF16), jax.ShapeDtypeStruct(shape, F32)],
        compiler_params=params(),
        name="add_extra",
    )(place, low, slots, table, table, table, table, send, keep)


def local(hidden, down_matrix, first_table, second_table, storage_index, request_adapter):
    steps, requests, units = hidden.shape
    per_shard, rank, all_units = first_table.shape
    features = second_table.shape[2]
    adapters = storage_index.shape[0]
    devices = all_units // units
    planes = devices // PLANE
    width = features // devices
    me = lax.axis_index("tensor").astype(jnp.int32)
    z, w = me // PLANE, me % PLANE
    place = jnp.stack([z, w])

    def in_plane(value, other):
        return lax.ppermute(value, "tensor", [(t, t ^ other) for t in range(devices)])

    def along(value, other):
        return lax.ppermute(value, "tensor", [(t, t ^ (other * PLANE)) for t in range(devices)])

    def hop(value, moves):
        pairs = [(a * PLANE + v, b * PLANE + v) for a, b in moves for v in range(PLANE)]
        return lax.ppermute(value, "tensor", pairs)

    table = jnp.arange(adapters, dtype=jnp.int32)
    slot_row = jnp.sum(
        jnp.where(request_adapter[:, None] == table[None, :], storage_index[None, :], 0), axis=1
    ).astype(jnp.int32)

    first = first_table.reshape(per_shard * rank, all_units)
    second = second_table.reshape(per_shard * rank, features)

    packed = pack_factors(place, first, planes, units)
    received = [in_plane(packed[o - 1], o) for o in range(1, PLANE)]

    if planes == 4:
        inner = (z == 1) | (z == 2)
        near = along(hidden, 1)
        middle = hop(hidden, ((1, 2), (2, 1)))
        order = jnp.stack([z, z ^ 1, jnp.where(z < 2, 2, 1), jnp.where(z < 2, 3, 0)])
        gathered = []
        for a, b in LOW_CHUNKS:
            outer_one = hop(middle[a:b], ((1, 0), (2, 3)))
            middle_two = hop(near[a:b], ((1, 2), (2, 1)))
            outer_two = hop(middle_two, ((1, 0), (2, 3)))
            gathered.append(
                [
                    hidden[a:b],
                    near[a:b],
                    jnp.where(inner, middle[a:b], outer_one),
                    jnp.where(inner, middle_two, outer_two),
                ]
            )
    else:
        order = jnp.stack([z ^ o for o in range(planes)])
        blocks = [hidden] + [along(hidden, o) for o in range(1, planes)]
        gathered = [[block[a:b] for block in blocks] for a, b in LOW_CHUNKS]

    send, keep = base_blocks(place, hidden, down_matrix, planes, width)

    lows = []
    for (a, b), blocks in zip(LOW_CHUNKS, gathered):
        slots = jnp.tile(slot_row[None, :], (1, b - a))
        low = low_part(place, order, slots, first, received, blocks, per_shard, rank)
        low = low + in_plane(low, 1)
        low = low + in_plane(low, 2)
        lows.append(low)

    outputs = []
    for a, b in SUM_CHUNKS:
        for (la, lb), low in zip(LOW_CHUNKS, lows):
            if la <= a and b <= lb:
                part = low[:, (a - la) * requests : (b - la) * requests]
        slots = jnp.tile(slot_row[None, :], (1, b - a))
        sent, kept = add_extra(place, part, slots, second, send, keep, (a, b), per_shard, rank)
        total = kept + in_plane(sent, 1).astype(F32)
        half = total[0] + in_plane(total[1].astype(BF16), 2).astype(F32)
        value = half[0]
        for o in range(1, planes):
            value = value + along(half[o].astype(BF16), o).astype(F32)
        outputs.append(value.astype(BF16).reshape(b - a, requests, width))
    return jnp.concatenate(outputs, axis=0)


def solution(mesh):
    in_specs = (
        P(None, "groups", "tensor"),
        P("tensor", None),
        P(("groups", "tensor"), None, None),
        P(("groups", "tensor"), None, None),
        P("groups"),
        P("groups"),
    )
    out_specs = P(None, "groups", "tensor")
    return jax.shard_map(local, mesh=mesh, in_specs=in_specs, out_specs=out_specs, check_vma=False)
```

```python
import jax
import jax.numpy as jnp
from jax import lax
from jax.experimental import pallas as pl
from jax.experimental.pallas import tpu as pltpu
from jax.sharding import PartitionSpec as P

PLANE = 4
F32 = jnp.float32
BF16 = jnp.bfloat16
VMEM_BYTES = 48 * 1024 * 1024
LOW_CHUNKS = ((0, 2), (2, 4))
SUM_CHUNKS = ((0, 2), (2, 3), (3, 4))


def halving(i, planes):
    out, bit = 0, 1
    while bit < planes:
        out = out * 2 + ((i // bit) % 2)
        bit *= 2
    return out


def after(value, *others):
    return lax.optimization_barrier((value, *others))[0]


def cost(flops, moved):
    return pl.CostEstimate(flops=int(flops) // 1000, bytes_accessed=int(moved) // 1000, transcendentals=0)


def hbm(*values):
    return [pltpu.with_memory_space_constraint(value, pltpu.HBM) for value in values]


def params():
    return pltpu.CompilerParams(vmem_limit_bytes=VMEM_BYTES)


def pack_factors(place, order, table, width, others, first, last):
    rows = table.shape[0]
    count = len(others)
    planes = last - first

    def body(place_ref, order_ref, *refs):
        for i in range(count):
            refs[count + i][0] = refs[i][...]

    def columns(other):
        return lambda i, p, o: (0, o[first + i] * PLANE + (p[1] ^ other))

    return pl.pallas_call(
        body,
        grid_spec=pltpu.PrefetchScalarGridSpec(
            num_scalar_prefetch=2,
            grid=(planes,),
            in_specs=[pl.BlockSpec((rows, width), columns(o)) for o in others],
            out_specs=[pl.BlockSpec((1, rows, width), lambda i, p, o: (i, 0, 0))] * count,
        ),
        out_shape=[jax.ShapeDtypeStruct((planes, rows, width), BF16)] * count,
        cost_estimate=cost(0, 4 * count * planes * rows * width),
        compiler_params=params(),
        name="pack_factors",
    )(place, order, *hbm(*([table] * count)))


def pack_core(place, order, first, second, width):
    rows, units = first.shape[0], 2 * width
    planes = first.shape[1] // (PLANE * units)

    def body(place_ref, order_ref, a_ref, s0_ref, s1_ref, out_ref):
        out_ref[0, 0] = a_ref[...]
        out_ref[1, 0, :, :width] = s0_ref[...]
        out_ref[1, 0, :, width:] = s1_ref[...]

    def columns(side):
        return lambda i, p, o: (
            0,
            (p[0] ^ halving(i, planes)) * PLANE + (p[1] ^ 1 ^ (2 * side)),
        )

    return pl.pallas_call(
        body,
        grid_spec=pltpu.PrefetchScalarGridSpec(
            num_scalar_prefetch=2,
            grid=(planes,),
            in_specs=[pl.BlockSpec((rows, units), lambda i, p, o: (0, o[i] * PLANE + (p[1] ^ 1)))]
            + [pl.BlockSpec((rows, width), columns(side)) for side in (0, 1)],
            out_specs=pl.BlockSpec((2, 1, rows, units), lambda i, p, o: (0, i, 0, 0)),
        ),
        out_shape=jax.ShapeDtypeStruct((2, planes, rows, units), BF16),
        cost_estimate=cost(0, 8 * planes * rows * units),
        compiler_params=params(),
        name="pack_core",
    )(place, order, *hbm(first, second, second))


def base_blocks(place, hidden, down, planes, width):
    steps, rows, units = hidden.shape

    def body(place_ref, hidden_ref, d0, d1, d2, d3, send_ref, keep_ref):
        flat = hidden_ref[...].reshape(steps * rows, units)
        for i, ref in enumerate((d0, d1, d2, d3)):
            value = jnp.dot(flat, ref[...], preferred_element_type=F32).reshape(steps, rows, width)
            if i & 1:
                send_ref[i >> 1, 0] = value.astype(BF16)
            else:
                keep_ref[i >> 1, 0] = value

    def columns(other):
        return lambda i, p: (0, (p[0] ^ halving(i, planes)) * PLANE + (p[1] ^ other))

    shape = (2, planes, steps, rows, width)
    return pl.pallas_call(
        body,
        grid_spec=pltpu.PrefetchScalarGridSpec(
            num_scalar_prefetch=1,
            grid=(planes,),
            in_specs=[pl.BlockSpec((steps, rows, units), lambda i, p: (0, 0, 0))]
            + [pl.BlockSpec((units, width), columns(o)) for o in range(PLANE)],
            out_specs=[pl.BlockSpec((2, 1, steps, rows, width), lambda i, p: (0, i, 0, 0, 0))] * 2,
        ),
        out_shape=[jax.ShapeDtypeStruct(shape, BF16), jax.ShapeDtypeStruct(shape, F32)],
        cost_estimate=cost(
            2 * steps * rows * units * down.shape[1], (2 * units + 3 * steps * rows) * down.shape[1]
        ),
        compiler_params=params(),
        name="base_blocks",
    )(place, *hbm(hidden, down, down, down, down))


def low_part(place, order, slots, tables, sources, first_plane, chunk, per_shard, rank):
    planes = len(sources)
    first_step, last_step = chunk
    steps = last_step - first_step
    rows, (_, requests, width) = tables[-1].shape[-2], sources[0][0].shape
    lanes = steps * requests
    hidden = [array for source in sources for array in source]

    def body(place_ref, order_ref, slots_ref, *refs):
        factor_refs, hidden_refs = refs[:PLANE], refs[PLANE : PLANE + len(hidden)]
        out_ref, held, factors, total = refs[PLANE + len(hidden) :]
        j = pl.program_id(0)
        at = 0
        for i, source in enumerate(sources):
            for inner in range(len(source)):
                chosen = j == i
                if len(source) > 1:
                    chosen &= place_ref[2] == 1 - inner

                @pl.when(chosen)
                def _(ref=hidden_refs[at]):
                    held[...] = ref[...].reshape(lanes, width)

                at += 1

        @pl.when(j == 0)
        def _():
            total[...] = jnp.zeros_like(total)

        for i, ref in enumerate(factor_refs):
            factors[i * rows : (i + 1) * rows, :] = ref[...].reshape(rows, width)
        total[...] += lax.dot_general(
            factors[...], held[...], (((1,), (1,)), ((), ())), preferred_element_type=F32
        )

        @pl.when(j == planes - 1)
        def _():
            low = jnp.zeros((rank, lanes), F32)
            wanted = slots_ref[...]
            for i in range(PLANE):
                first = (place_ref[0] * PLANE + (place_ref[1] ^ i)) * per_shard
                for a in range(per_shard):
                    at = (i * per_shard + a) * rank
                    low += jnp.where(wanted == first + a, total[at : at + rank, :], 0.0)
            out_ref[...] = low

    def hidden_spec(array):
        block = first_step // steps if array.shape[0] > steps else 0
        return pl.BlockSpec((steps, requests, width), lambda j, p, o: (block, 0, 0))

    return pl.pallas_call(
        body,
        grid_spec=pltpu.PrefetchScalarGridSpec(
            num_scalar_prefetch=2,
            grid=(planes,),
            in_specs=[
                pl.BlockSpec((1, lanes), lambda j, p, o: (0, 0)),
                pl.BlockSpec((rows, width), lambda j, p, o: (0, o[first_plane + j] * PLANE + p[1])),
                pl.BlockSpec((1, 1, rows, width), lambda j, p, o: (0, first_plane + j, 0, 0)),
                pl.BlockSpec((1, rows, width), lambda j, p, o: (j, 0, 0)),
                pl.BlockSpec((1, rows, width), lambda j, p, o: (j, 0, 0)),
                *[hidden_spec(array) for array in hidden],
            ],
            out_specs=pl.BlockSpec((rank, lanes), lambda j, p, o: (0, 0)),
            scratch_shapes=[
                pltpu.VMEM((lanes, width), BF16),
                pltpu.VMEM((PLANE * rows, width), BF16),
                pltpu.VMEM((PLANE * rows, lanes), F32),
            ],
        ),
        out_shape=jax.ShapeDtypeStruct((rank, lanes), F32),
        cost_estimate=cost(
            2 * lanes * PLANE * rows * planes * width, 2 * (lanes + PLANE * rows) * planes * width
        ),
        compiler_params=params(),
        name="low_part",
    )(place, order, slots, *hbm(*tables, *hidden))


def add_extra(place, low, slots, mine, other, keep, recv, chunk, side, per_shard, rank):
    _, planes, _, requests, width = keep.shape
    first_step, last_step = chunk
    steps = last_step - first_step
    lanes = steps * requests
    rows = mine.shape[0]
    kind = BF16 if side else F32

    def body(place_ref, low_ref, slots_ref, *refs):
        tables, (t_ref, k_ref, r_ref, out_ref) = refs[:planes], refs[planes:]
        rounded = low_ref[...].astype(BF16).astype(F32)
        wanted = slots_ref[...]
        spread = []
        for i in range(2):
            first = (place_ref[0] * PLANE + (place_ref[1] ^ i)) * per_shard
            parts = [jnp.where(wanted == first + a, rounded, 0.0) for a in range(per_shard)]
            spread.append(jnp.concatenate(parts, axis=0).T.astype(BF16))
        for i in range(planes):
            extra = jnp.dot(spread[0], tables[i][...], preferred_element_type=F32)
            extra += jnp.dot(spread[1], t_ref[0, i], preferred_element_type=F32)
            base = k_ref[0, i] + r_ref[0, i].astype(F32)
            out_ref[i] = (base.reshape(lanes, width) + extra).astype(kind)

    def columns(i):
        return lambda j, p: (0, (p[0] ^ halving(i, planes)) * PLANE + (p[1] ^ (2 * side)))

    blocks = [pl.BlockSpec((rows, width), columns(i)) for i in range(planes)]
    base = pl.BlockSpec(
        (1, planes, steps, requests, width), lambda i, p: (side, 0, first_step // steps, 0, 0)
    )
    return pl.pallas_call(
        body,
        grid_spec=pltpu.PrefetchScalarGridSpec(
            num_scalar_prefetch=1,
            grid=(1,),
            in_specs=[
                pl.BlockSpec((rank, lanes), lambda i, p: (0, 0)),
                pl.BlockSpec((1, lanes), lambda i, p: (0, 0)),
                *blocks,
                pl.BlockSpec((1, planes, rows, width), lambda i, p: (1, 0, 0, side)),
                base,
                base,
            ],
            out_specs=pl.BlockSpec((planes, lanes, width), lambda i, p: (0, 0, 0)),
        ),
        out_shape=jax.ShapeDtypeStruct((planes, lanes, width), kind),
        cost_estimate=cost(4 * lanes * rows * planes * width, 10 * lanes * planes * width),
        compiler_params=params(),
        name="add_extra",
    )(place, low, slots, *hbm(*([mine] * planes), other, keep, recv))


def local(hidden, down_matrix, first_table, second_table, storage_index, request_adapter):
    steps, requests, units = hidden.shape
    per_shard, rank, all_units = first_table.shape
    features = second_table.shape[2]
    adapters = storage_index.shape[0]
    devices = all_units // units
    planes = devices // PLANE
    width = features // devices
    me = lax.axis_index("tensor").astype(jnp.int32)
    z, w = me // PLANE, me % PLANE
    place = jnp.stack([z, w, ((z == 1) | (z == 2)).astype(jnp.int32)])

    def in_plane(value, other):
        return lax.ppermute(value, "tensor", [(t, t ^ other) for t in range(devices)])

    def along(value, other):
        return lax.ppermute(value, "tensor", [(t, t ^ (other * PLANE)) for t in range(devices)])

    def hop(value, moves):
        pairs = [(a * PLANE + v, b * PLANE + v) for a, b in moves for v in range(PLANE)]
        return lax.ppermute(value, "tensor", pairs)

    table = jnp.arange(adapters, dtype=jnp.int32)
    slot_row = jnp.sum(
        jnp.where(request_adapter[:, None] == table[None, :], storage_index[None, :], 0), axis=1
    ).astype(jnp.int32)

    first = first_table.reshape(per_shard * rank, all_units)
    second = second_table.reshape(per_shard * rank, features)

    if planes == 4:
        order = jnp.stack([z, z ^ 1, jnp.where(z < 2, 2, 1), jnp.where(z < 2, 3, 0)])
    else:
        order = jnp.stack([z ^ o for o in range(planes)])
    split = planes // 2

    for_y = pack_factors(place, order, first, units, (2, 3), 0, split)
    near_y = [in_plane(block, o) for block, o in zip(for_y, (2, 3))]
    hidden_z = after(hidden, *for_y)
    if planes == 4:
        near = along(hidden_z, 1)
        middle = hop(hidden_z, ((1, 2), (2, 1)))
    else:
        blocks = [hidden] + [along(hidden_z, o) for o in range(1, planes)]
        near = middle = blocks[1]
    for_far = pack_factors(place, order, after(first, *for_y), units, (2, 3), split, planes)
    for_core = pack_core(place, order, after(first, *for_far), second, width)
    send, keep = base_blocks(place, after(hidden, for_core), down_matrix, planes, width)
    near, middle, send, *near_y = lax.optimization_barrier((near, middle, send, *near_y))
    from_core = in_plane(after(for_core, near), 1)
    far_y = [in_plane(after(for_far[0], *near_y), 2)]
    far_y.append(in_plane(after(for_far[1], *far_y), 3))

    if planes == 4:
        gathered = []
        near_rest, middle_rest = near, middle
        for a, b in LOW_CHUNKS:
            outer_one = hop(middle_rest[a:b], ((1, 0), (2, 3)))
            middle_two = hop(near_rest[a:b], ((1, 2), (2, 1)))
            ready = after(middle_two, outer_one, far_y[0])
            if a == 0:
                recv = in_plane(after(send, outer_one, middle_two), 1)
            outer_two = hop(ready, ((1, 0), (2, 3)))
            near_rest = after(near, middle_two)
            middle_rest = after(middle, outer_two, *far_y)
            gathered.append([[middle, outer_one], [middle_two, outer_two]])
        second_wave = [source[1] for source in gathered[1]]
    else:
        gathered = [[[block] for block in blocks[split:]] for _ in LOW_CHUNKS]
        recv = in_plane(send, 1)
        second_wave = []
    at_hand = [[hidden], [near]] if planes == 4 else [[block] for block in blocks[:split]]
    slots = jnp.tile(slot_row[None, :], (1, steps))
    early = low_part(
        place, order, slots, (first, from_core, *near_y), at_hand, 0, (0, steps), per_shard, rank
    )

    def low_of(chunk, sources, token):
        a, b = chunk
        tables = (first, after(from_core, early, *token), *far_y)
        sources = [[after(array, *token) for array in source] for source in sources]
        low = low_part(
            place, order, slots[:, a * requests : b * requests], tables, sources, split, chunk, per_shard, rank
        )
        low = low + early[:, a * requests : b * requests]
        low = low + in_plane(low, 1)
        return low + in_plane(low, 2)

    def blocks_of(low, low_chunk, chunk, side):
        (a, _), (c, d) = low_chunk, chunk
        part = low[:, (c - a) * requests : (d - a) * requests]
        slots = jnp.tile(slot_row[None, :], (1, d - c))
        return add_extra(
            place, part, slots, second, from_core, keep, recv, chunk, side, per_shard, rank
        )

    def begin(low, low_chunk):
        begun = []
        for chunk in SUM_CHUNKS:
            if low_chunk[0] <= chunk[0] and chunk[1] <= low_chunk[1]:
                sent = blocks_of(low, low_chunk, chunk, 1)
                begun.append([low_chunk, chunk, low, in_plane(sent, 2)])
                low = after(low, sent)
        return begun

    def stay(low_chunk, chunk, low, token):
        return blocks_of(after(low, *token), low_chunk, chunk, 0)

    low = low_of(LOW_CHUNKS[0], gathered[0], ())
    begun = begin(after(low, *second_wave[:1]), LOW_CHUNKS[0])
    token = tuple(b[2] for b in begun)
    for chunk, sources in zip(LOW_CHUNKS[1:], gathered[1:]):
        low = low_of(chunk, sources, token)
        begun += begin(low, chunk)
    token = (begun[-1][2],)
    stages = planes.bit_length()
    events = sorted((3 * c + 2 * s, c, s) for c in range(len(SUM_CHUNKS)) for s in range(stages))
    state = []
    for _, c, stage in events:
        if stage == 0:
            low_chunk, chunk, low, received = begun[c]
            value = stay(low_chunk, chunk, low, token)
            token = (value,)
        else:
            value, received = state[c]
        half = value + after(received, *token).astype(F32)
        if stage == 0:
            state.append(None)
        if stage == stages - 1:
            state[c] = (half, None)
            token = (half,)
        else:
            count = half.shape[0] // 2
            moving = half[count:].astype(BF16)
            state[c] = (half[:count], along(moving, 1 << stage))
            token = (moving,)
    outputs = [
        value[0].astype(BF16).reshape(d - c, requests, width)
        for (value, _), (c, d) in zip(state, SUM_CHUNKS)
    ]
    return jnp.concatenate(outputs, axis=0)


def solution(mesh):
    in_specs = (
        P(None, "groups", "tensor"),
        P("tensor", None),
        P(("groups", "tensor"), None, None),
        P(("groups", "tensor"), None, None),
        P("groups"),
        P("groups"),
    )
    out_specs = P(None, "groups", "tensor")
    return jax.shard_map(local, mesh=mesh, in_specs=in_specs, out_specs=out_specs, check_vma=False)
```

```python
import jax
import jax.numpy as jnp
from jax import lax
from jax.experimental import pallas as pl
from jax.experimental.pallas import tpu as pltpu
from jax.sharding import PartitionSpec as P

PLANE = 4
F32 = jnp.float32
BF16 = jnp.bfloat16
VMEM_BYTES = 48 * 1024 * 1024
LOW_CHUNKS = ((0, 2), (2, 4))
KEEP_Y, SEND_Y, KEEP_Z, SEND_Z = range(4)


def halving(i, planes):
    out, bit = 0, 1
    while bit < planes:
        out = out * 2 + ((i // bit) % 2)
        bit *= 2
    return out


def after(value, *others):
    return lax.optimization_barrier((value, *others))[0]


def cost(flops, moved, share=1000):
    return pl.CostEstimate(
        flops=int(flops) // share, bytes_accessed=int(moved) // share, transcendentals=0
    )


def hbm(*values):
    return [pltpu.with_memory_space_constraint(value, pltpu.HBM) for value in values]


def params():
    return pltpu.CompilerParams(vmem_limit_bytes=VMEM_BYTES)


def pack_factors(place, order, table, width, other):
    rows = table.shape[0]
    planes = table.shape[1] // (PLANE * width)

    def body(place_ref, order_ref, *refs):
        for i in range(planes):
            refs[planes][i] = refs[i][...]

    def columns(i):
        return lambda j, p, o: (0, o[i] * PLANE + (p[1] ^ other))

    return pl.pallas_call(
        body,
        grid_spec=pltpu.PrefetchScalarGridSpec(
            num_scalar_prefetch=2,
            grid=(1,),
            in_specs=[pl.BlockSpec((rows, width), columns(i)) for i in range(planes)],
            out_specs=pl.BlockSpec((planes, rows, width), lambda i, p, o: (0, 0, 0)),
        ),
        out_shape=jax.ShapeDtypeStruct((planes, rows, width), BF16),
        cost_estimate=cost(0, 4 * planes * rows * width),
        compiler_params=params(),
        name="pack_factors",
    )(place, order, *hbm(*([table] * planes)))


def pack_core(place, order, first, second, width):
    rows, units = first.shape[0], 2 * width
    planes = first.shape[1] // (PLANE * units)

    def body(place_ref, order_ref, a_ref, s0_ref, s1_ref, out_ref):
        out_ref[0, 0] = a_ref[...]
        out_ref[1, 0, :, :width] = s0_ref[...]
        out_ref[1, 0, :, width:] = s1_ref[...]

    def columns(side):
        return lambda i, p, o: (
            0,
            (p[0] ^ halving(i, planes)) * PLANE + (p[1] ^ 1 ^ (2 * side)),
        )

    return pl.pallas_call(
        body,
        grid_spec=pltpu.PrefetchScalarGridSpec(
            num_scalar_prefetch=2,
            grid=(planes,),
            in_specs=[pl.BlockSpec((rows, units), lambda i, p, o: (0, o[i] * PLANE + (p[1] ^ 1)))]
            + [pl.BlockSpec((rows, width), columns(side)) for side in (0, 1)],
            out_specs=pl.BlockSpec((2, 1, rows, units), lambda i, p, o: (0, i, 0, 0)),
        ),
        out_shape=jax.ShapeDtypeStruct((2, planes, rows, units), BF16),
        cost_estimate=cost(0, 8 * planes * rows * units),
        compiler_params=params(),
        name="pack_core",
    )(place, order, *hbm(first, second, second))


def base_blocks(place, hidden, down, planes, width):
    steps, rows, units = hidden.shape

    def body(place_ref, hidden_ref, d0, d1, d2, d3, send_ref, keep_ref):
        flat = hidden_ref[...].reshape(steps * rows, units)
        for i, ref in enumerate((d0, d1, d2, d3)):
            value = jnp.dot(flat, ref[...], preferred_element_type=F32).reshape(steps, rows, width)
            if i & 1:
                send_ref[i >> 1, 0] = value.astype(BF16)
            else:
                keep_ref[i >> 1, 0] = value

    def columns(other):
        return lambda i, p: (0, (p[0] ^ halving(i, planes)) * PLANE + (p[1] ^ other))

    shape = (2, planes, steps, rows, width)
    return pl.pallas_call(
        body,
        grid_spec=pltpu.PrefetchScalarGridSpec(
            num_scalar_prefetch=1,
            grid=(planes,),
            in_specs=[pl.BlockSpec((steps, rows, units), lambda i, p: (0, 0, 0))]
            + [pl.BlockSpec((units, width), columns(o)) for o in range(PLANE)],
            out_specs=[pl.BlockSpec((2, 1, steps, rows, width), lambda i, p: (0, i, 0, 0, 0))] * 2,
        ),
        out_shape=[jax.ShapeDtypeStruct(shape, BF16), jax.ShapeDtypeStruct(shape, F32)],
        cost_estimate=cost(
            2 * steps * rows * units * down.shape[1], (2 * units + 3 * steps * rows) * down.shape[1]
        ),
        compiler_params=params(),
        name="base_blocks",
    )(place, *hbm(hidden, down, down, down, down))


def low_part(place, order, slots, owners, tables, sources, first_plane, chunk, per_shard, rank):
    planes = len(sources)
    first_step, last_step = chunk
    steps = last_step - first_step
    rows, (_, requests, width) = tables[-1].shape[-2], sources[0][0].shape
    lanes, count = steps * requests, len(owners)
    hidden = [array for source in sources for array in source]

    def body(place_ref, order_ref, slots_ref, *refs):
        factor_refs, hidden_refs = refs[:count], refs[count : count + len(hidden)]
        out_ref, held, factors, total = refs[count + len(hidden) :]
        j = pl.program_id(0)
        at = 0
        for i, source in enumerate(sources):
            for inner in range(len(source)):
                chosen = j == i
                if len(source) > 1:
                    chosen &= place_ref[2] == 1 - inner

                @pl.when(chosen)
                def _(ref=hidden_refs[at]):
                    held[...] = ref[...].reshape(lanes, width)

                at += 1

        @pl.when(j == 0)
        def _():
            total[...] = jnp.zeros_like(total)

        for i, ref in enumerate(factor_refs):
            factors[i * rows : (i + 1) * rows, :] = ref[...].reshape(rows, width)
        total[...] += lax.dot_general(
            factors[...], held[...], (((1,), (1,)), ((), ())), preferred_element_type=F32
        )

        @pl.when(j == planes - 1)
        def _():
            low = jnp.zeros((rank, lanes), F32)
            wanted = slots_ref[...]
            for i, owner in enumerate(owners):
                first = (place_ref[0] * PLANE + (place_ref[1] ^ owner)) * per_shard
                for a in range(per_shard):
                    at = (i * per_shard + a) * rank
                    low += jnp.where(wanted == first + a, total[at : at + rank, :], 0.0)
            out_ref[...] = low

    def factor_spec(owner):
        if owner == 0:
            return pl.BlockSpec(
                (rows, width), lambda j, p, o: (0, o[first_plane + j] * PLANE + p[1])
            )
        if owner == 1:
            return pl.BlockSpec((1, 1, rows, width), lambda j, p, o: (0, first_plane + j, 0, 0))
        return pl.BlockSpec((1, rows, width), lambda j, p, o: (first_plane + j, 0, 0))

    def hidden_spec(array):
        block = first_step // steps if array.shape[0] > steps else 0
        return pl.BlockSpec((steps, requests, width), lambda j, p, o: (block, 0, 0))

    return pl.pallas_call(
        body,
        grid_spec=pltpu.PrefetchScalarGridSpec(
            num_scalar_prefetch=2,
            grid=(planes,),
            in_specs=[
                pl.BlockSpec((1, lanes), lambda j, p, o: (0, 0)),
                *[factor_spec(owner) for owner in owners],
                *[hidden_spec(array) for array in hidden],
            ],
            out_specs=pl.BlockSpec((rank, lanes), lambda j, p, o: (0, 0)),
            scratch_shapes=[
                pltpu.VMEM((lanes, width), BF16),
                pltpu.VMEM((count * rows, width), BF16),
                pltpu.VMEM((count * rows, lanes), F32),
            ],
        ),
        out_shape=jax.ShapeDtypeStruct((rank, lanes), F32),
        cost_estimate=cost(
            2 * lanes * count * rows * planes * width, 2 * (lanes + count * rows) * planes * width, 1
        ),
        compiler_params=params(),
        name="low_part",
    )(place, order, slots, *hbm(*tables, *hidden))


def add_extra(place, low, slots, mine, other, keep, recv, first_step, pieces, per_shard, rank):
    _, planes, _, requests, width = keep.shape
    rows, lanes = mine.shape[0], low.shape[1]
    count, half = len(pieces), planes // 2
    parts = {
        KEEP_Y: ((0,), range(planes)),
        SEND_Y: ((1,), range(planes)),
        KEEP_Z: ((0, 1), range(half)),
        SEND_Z: ((0, 1), range(half, planes)),
    }
    sides = sorted({side for _, what in pieces for side in parts[what][0]})

    def body(place_ref, low_ref, slots_ref, *refs):
        tables, refs = refs[: len(sides) * planes], refs[len(sides) * planes :]
        others, refs = refs[: len(sides)], refs[len(sides) :]
        rounded = low_ref[...].astype(BF16).astype(F32)
        wanted = slots_ref[...]
        spread = []
        for i in range(2):
            first = (place_ref[0] * PLANE + (place_ref[1] ^ i)) * per_shard
            masked = [jnp.where(wanted == first + a, rounded, 0.0) for a in range(per_shard)]
            spread.append(jnp.concatenate(masked, axis=0).T.astype(BF16))
        for n, (step, what) in enumerate(pieces):
            k_ref, r_ref, out_ref = refs[n], refs[count + n], refs[2 * count + n]
            start = (step - first_step) * requests
            here = [value[start : start + requests] for value in spread]
            for side_at, side in enumerate(parts[what][0]):
                at = sides.index(side)
                for block_at, i in enumerate(parts[what][1]):
                    extra = jnp.dot(
                        here[0], tables[at * planes + i][...], preferred_element_type=F32
                    )
                    extra += jnp.dot(here[1], others[at][0, i], preferred_element_type=F32)
                    base = k_ref[side_at, block_at, 0] + r_ref[side_at, block_at, 0].astype(F32)
                    out_ref[side_at, block_at] = (base + extra).astype(out_ref.dtype)

    def columns(i, side):
        return lambda j, p: (0, (p[0] ^ halving(i, planes)) * PLANE + (p[1] ^ (2 * side)))

    def shape(what):
        return (len(parts[what][0]), len(parts[what][1]), requests, width)

    def base(step, what):
        side = 1 if what == SEND_Y else 0
        block = 1 if what == SEND_Z else 0
        n, m, _, _ = shape(what)
        return pl.BlockSpec((n, m, 1, requests, width), lambda i, p: (side, block, step, 0, 0))

    def other_spec(side):
        return pl.BlockSpec((1, planes, rows, width), lambda i, p: (1, 0, 0, side))

    bases = [base(*piece) for piece in pieces]
    return pl.pallas_call(
        body,
        grid_spec=pltpu.PrefetchScalarGridSpec(
            num_scalar_prefetch=1,
            grid=(1,),
            in_specs=[
                pl.BlockSpec((rank, lanes), lambda i, p: (0, 0)),
                pl.BlockSpec((1, lanes), lambda i, p: (0, 0)),
                *[
                    pl.BlockSpec((rows, width), columns(i, side))
                    for side in sides
                    for i in range(planes)
                ],
                *[other_spec(side) for side in sides],
                *bases,
                *bases,
            ],
            out_specs=[pl.BlockSpec(shape(what), lambda i, p: (0, 0, 0, 0)) for _, what in pieces],
        ),
        out_shape=[
            jax.ShapeDtypeStruct(shape(what), BF16 if what in (SEND_Y, SEND_Z) else F32)
            for _, what in pieces
        ],
        cost_estimate=cost(4 * lanes * rows * planes * width, 10 * lanes * planes * width),
        compiler_params=params(),
        name="add_extra",
    )(
        place,
        low,
        slots,
        *hbm(*([mine] * (planes * len(sides))), *([other] * len(sides))),
        *hbm(*([keep] * count), *([recv] * count)),
    )


def local(hidden, down_matrix, first_table, second_table, storage_index, request_adapter):
    steps, requests, units = hidden.shape
    per_shard, rank, all_units = first_table.shape
    features = second_table.shape[2]
    adapters = storage_index.shape[0]
    devices = all_units // units
    planes = devices // PLANE
    width = features // devices
    me = lax.axis_index("tensor").astype(jnp.int32)
    z, w = me // PLANE, me % PLANE
    place = jnp.stack([z, w, ((z == 1) | (z == 2)).astype(jnp.int32)])

    def in_plane(value, other):
        return lax.ppermute(value, "tensor", [(t, t ^ other) for t in range(devices)])

    def along(value, other):
        return lax.ppermute(value, "tensor", [(t, t ^ (other * PLANE)) for t in range(devices)])

    def hop(value, moves):
        pairs = [(a * PLANE + v, b * PLANE + v) for a, b in moves for v in range(PLANE)]
        return lax.ppermute(value, "tensor", pairs)

    table = jnp.arange(adapters, dtype=jnp.int32)
    slot_row = jnp.sum(
        jnp.where(request_adapter[:, None] == table[None, :], storage_index[None, :], 0), axis=1
    ).astype(jnp.int32)

    first = first_table.reshape(per_shard * rank, all_units)
    second = second_table.reshape(per_shard * rank, features)

    if planes == 4:
        order = jnp.stack([z, z ^ 1, jnp.where(z < 2, 2, 1), jnp.where(z < 2, 3, 0)])
    else:
        order = jnp.stack([z ^ o for o in range(planes)])
    split = planes // 2

    for_near = pack_factors(place, order, first, units, 2)
    near_y = in_plane(for_near, 2)
    hidden_z = hidden
    if planes == 4:
        near = along(hidden_z, 1)
        middle = hop(hidden_z, ((1, 2), (2, 1)))
    else:
        blocks = [hidden] + [along(hidden_z, o) for o in range(1, planes)]
        near = middle = blocks[1]
    for_far = pack_factors(place, order, after(first, for_near), units, 3)
    for_core = pack_core(place, order, after(first, for_far), second, width)
    send, keep = base_blocks(place, after(hidden, for_core), down_matrix, planes, width)
    near, middle, send, near_y = lax.optimization_barrier((near, middle, send, near_y))
    from_core = in_plane(after(for_core, near), 1)
    far_y = in_plane(after(for_far, near_y), 3)
    recv = in_plane(send, 1)

    at_hand = [[hidden], [near]] if planes == 4 else [[block] for block in blocks[:split]]
    slots = jnp.tile(slot_row[None, :], (1, steps))

    def low_at(chunk, owners, tables, sources, first_plane):
        lanes = slots[:, chunk[0] * requests : chunk[1] * requests]
        return low_part(
            place, order, lanes, owners, tables, sources, first_plane, chunk, per_shard, rank
        )

    def early_of(*ready):
        near_by = (first, after(from_core, *ready), near_y)
        part = low_at((0, steps), (0, 1, 2), near_by, at_hand, 0)
        return part, low_at((0, steps), (3,), (after(far_y, part),), at_hand, 0)

    def late_of(chunk, plane, source, *ready):
        tables = (first, after(from_core, *ready), near_y, far_y)
        return low_at(chunk, range(PLANE), tables, [source], plane)

    if planes == 4:
        outward, across = ((1, 0), (2, 3)), ((1, 2), (2, 1))
        (a, b), (c, d) = LOW_CHUNKS
        outer_one = hop(middle[a:b], outward)
        middle_two = hop(near[a:b], across)
        outer_two = hop(after(middle_two, outer_one), outward)
        early, early_far = early_of(outer_one, middle_two)
        part = late_of((a, b), 2, [middle, outer_one], early_far)
        late = [[part, [middle_two, outer_two]]]
        middle_two = hop(after(near[c:d], middle_two), across)
        outer_one = hop(after(middle[c:d], outer_one), outward)
        outer_two = hop(after(middle_two, outer_two, part), outward)
        late.append([[middle, outer_one], [middle_two, outer_two]])
        second_wave = [outer_one]
    else:
        early, early_far = early_of()
        late = [[[block] for block in blocks[split:]] for _ in LOW_CHUNKS]
        second_wave = []

    def core_sum(chunk, parts):
        low = (early + early_far)[:, chunk[0] * requests : chunk[1] * requests]
        for part in parts:
            low = low + part
        return low + in_plane(low, 1)

    def with_extra(low, first_step, pieces):
        lanes = slots[:, : low.shape[1]]
        return add_extra(
            place, low, lanes, second, from_core, keep, recv, first_step, pieces, per_shard, rank
        )

    along_z = [1 << bit for bit in range(planes.bit_length() - 1)]
    y_first, z_first = ["y", *along_z], [*along_z[:1], "y", *along_z[1:]]
    plans = [list(plan) for plan in (y_first, z_first, y_first, z_first)]
    state = [None] * steps

    def send(value, stage):
        return in_plane(value, 2) if stage == "y" else along(value, stage)

    def add(c, *ready):
        value, received = state[c]
        total = value + after(received, *ready).astype(F32)
        plans[c].pop(0)
        if not plans[c]:
            state[c] = (total, None)
            return total
        count = total.shape[0] // 2
        stays, goes = total[:count], total[count:].astype(BF16)
        if plans[c][0] == "y":
            stays, goes = stays[0], goes[0]
        state[c] = (stays, send(goes, plans[c][0]))
        return goes

    def begin(c, stays, goes):
        if plans[c][0] == "y":
            stays, goes = stays[0], goes[0]
        state[c] = (stays, send(goes, plans[c][0]))

    parts, ready = [], early_far
    for i, source in enumerate(late[0]):
        part = late_of(LOW_CHUNKS[0], split + i, source, ready) if isinstance(source, list) else source
        parts.append(part)
        ready = part
    low = core_sum(LOW_CHUNKS[0], parts)
    low = low + in_plane(low, 2)
    (goes,) = with_extra(low[:, :requests], 0, [(0, SEND_Y)])
    low = after(low, goes, *second_wave)
    moved = send(goes[0], "y")
    stays, goes, next_stays = with_extra(low, 0, [(0, KEEP_Y), (1, SEND_Z), (1, KEEP_Z)])
    state[0] = (stays[0], moved)
    parts, ready = [], (stays, goes, next_stays)
    for i, source in enumerate(late[1]):
        source = [after(array, *ready) for array in source]
        parts.append(late_of(LOW_CHUNKS[1], split + i, source, *ready))
        ready = (parts[-1],)
    begin(1, next_stays, after(goes, parts[0]))

    low = core_sum(LOW_CHUNKS[1], parts)
    across_y = in_plane(low, 2)
    done = add(0, low)
    low = low + after(across_y, done)
    moved, stays, goes, next_stays = with_extra(
        low, 2, [(2, SEND_Y), (2, KEEP_Y), (3, SEND_Z), (3, KEEP_Z)]
    )
    begin(2, stays, moved)
    begin(3, next_stays, goes)
    done = next_stays
    for c in (1, 0, 2, 1, 3, 0, 2, 3, 1, 2, 3):
        if plans[c]:
            done = add(c, done)
    for c in range(steps):
        while plans[c]:
            done = add(c, done)
    outputs = [value.astype(BF16) for value, _ in state]
    return jnp.concatenate(outputs, axis=0)


def solution(mesh):
    in_specs = (
        P(None, "groups", "tensor"),
        P("tensor", None),
        P(("groups", "tensor"), None, None),
        P(("groups", "tensor"), None, None),
        P("groups"),
        P("groups"),
    )
    out_specs = P(None, "groups", "tensor")
    return jax.shard_map(local, mesh=mesh, in_specs=in_specs, out_specs=out_specs, check_vma=False)
```

```python
import jax
import jax.numpy as jnp
from jax import lax
from jax.experimental import pallas as pl
from jax.experimental.pallas import tpu as pltpu
from jax.sharding import PartitionSpec as P

PLANE = 4
F32 = jnp.float32
BF16 = jnp.bfloat16
LOW_CHUNKS = ((0, 2), (2, 4))
KEEP_Y, SEND_Y, KEEP_Z, SEND_Z = range(4)


def halving(i, planes):
    out, bit = 0, 1
    while bit < planes:
        out = out * 2 + ((i // bit) % 2)
        bit *= 2
    return out


def after(value, *others):
    return lax.optimization_barrier((value, *others))[0]


def cost(flops, moved, share=1000):
    return pl.CostEstimate(
        flops=int(flops) // share, bytes_accessed=int(moved) // share, transcendentals=0
    )


def hbm(*values):
    return [pltpu.with_memory_space_constraint(value, pltpu.HBM) for value in values]


def params(mebibytes):
    return pltpu.CompilerParams(vmem_limit_bytes=mebibytes * 1024 * 1024)


def pack_factors(place, order, table, width, other):
    rows = table.shape[0]
    planes = table.shape[1] // (PLANE * width)

    def body(place_ref, order_ref, *refs):
        for i in range(planes):
            refs[planes][i] = refs[i][...]

    def columns(i):
        return lambda j, p, o: (0, o[i] * PLANE + (p[1] ^ other))

    return pl.pallas_call(
        body,
        grid_spec=pltpu.PrefetchScalarGridSpec(
            num_scalar_prefetch=2,
            grid=(1,),
            in_specs=[pl.BlockSpec((rows, width), columns(i)) for i in range(planes)],
            out_specs=pl.BlockSpec((planes, rows, width), lambda i, p, o: (0, 0, 0)),
        ),
        out_shape=jax.ShapeDtypeStruct((planes, rows, width), BF16),
        cost_estimate=cost(0, 4 * planes * rows * width),
        compiler_params=params(10),
        name="pack_factors",
    )(place, order, *hbm(*([table] * planes)))


def pack_core(place, order, first, second, width):
    rows, units = first.shape[0], 2 * width
    planes = first.shape[1] // (PLANE * units)

    def body(place_ref, order_ref, a_ref, s0_ref, s1_ref, out_ref):
        out_ref[0, 0] = a_ref[...]
        out_ref[1, 0, :, :width] = s0_ref[...]
        out_ref[1, 0, :, width:] = s1_ref[...]

    def columns(side):
        return lambda i, p, o: (
            0,
            (p[0] ^ halving(i, planes)) * PLANE + (p[1] ^ 1 ^ (2 * side)),
        )

    return pl.pallas_call(
        body,
        grid_spec=pltpu.PrefetchScalarGridSpec(
            num_scalar_prefetch=2,
            grid=(planes,),
            in_specs=[pl.BlockSpec((rows, units), lambda i, p, o: (0, o[i] * PLANE + (p[1] ^ 1)))]
            + [pl.BlockSpec((rows, width), columns(side)) for side in (0, 1)],
            out_specs=pl.BlockSpec((2, 1, rows, units), lambda i, p, o: (0, i, 0, 0)),
        ),
        out_shape=jax.ShapeDtypeStruct((2, planes, rows, units), BF16),
        cost_estimate=cost(0, 8 * planes * rows * units),
        compiler_params=params(10),
        name="pack_core",
    )(place, order, *hbm(first, second, second))


def base_blocks(place, hidden, down, planes, width):
    steps, rows, units = hidden.shape

    def body(place_ref, hidden_ref, d0, d1, d2, d3, send_ref, keep_ref):
        flat = hidden_ref[...].reshape(steps * rows, units)
        for i, ref in enumerate((d0, d1, d2, d3)):
            value = jnp.dot(flat, ref[...], preferred_element_type=F32).reshape(steps, rows, width)
            if i & 1:
                send_ref[i >> 1, 0] = value.astype(BF16)
            else:
                keep_ref[i >> 1, 0] = value

    def columns(other):
        return lambda i, p: (0, (p[0] ^ halving(i, planes)) * PLANE + (p[1] ^ other))

    shape = (2, planes, steps, rows, width)
    return pl.pallas_call(
        body,
        grid_spec=pltpu.PrefetchScalarGridSpec(
            num_scalar_prefetch=1,
            grid=(planes,),
            in_specs=[pl.BlockSpec((steps, rows, units), lambda i, p: (0, 0, 0))]
            + [pl.BlockSpec((units, width), columns(o)) for o in range(PLANE)],
            out_specs=[pl.BlockSpec((2, 1, steps, rows, width), lambda i, p: (0, i, 0, 0, 0))] * 2,
        ),
        out_shape=[jax.ShapeDtypeStruct(shape, BF16), jax.ShapeDtypeStruct(shape, F32)],
        cost_estimate=cost(
            2 * steps * rows * units * down.shape[1], (2 * units + 3 * steps * rows) * down.shape[1]
        ),
        compiler_params=params(24),
        name="base_blocks",
    )(place, *hbm(hidden, down, down, down, down))


def low_part(place, slots, owners, tables, sources, first_plane, chunk, per_shard, rank, share):
    first_step, last_step = chunk
    steps = last_step - first_step
    rows, (_, requests, width) = tables[-1].shape[-2], sources[0][0].shape
    lanes, count = steps * requests, len(owners)
    hidden = [array for source in sources for array in source]

    def body(place_ref, slots_ref, *refs):
        factor_refs, hidden_refs = refs[:count], refs[count : count + len(hidden)]
        out_ref, held, factors = refs[count + len(hidden) :]
        total, at = None, 0
        for j, source in enumerate(sources):
            for inner in range(len(source)):
                ref = hidden_refs[at]
                start = first_step if ref.shape[0] > steps else 0
                if len(source) == 1:
                    held[...] = ref[start : start + steps].reshape(lanes, width)
                else:

                    @pl.when(place_ref[2] == 1 - inner)
                    def _(ref=ref, start=start):
                        held[...] = ref[start : start + steps].reshape(lanes, width)

                at += 1
            for i, ref in enumerate(factor_refs):
                factors[i * rows : (i + 1) * rows, :] = (
                    ref[0, first_plane + j] if ref.shape[0] == 2 else ref[first_plane + j]
                )
            product = lax.dot_general(
                factors[...], held[...], (((1,), (1,)), ((), ())), preferred_element_type=F32
            )
            total = product if total is None else total + product
        low = jnp.zeros((rank, lanes), F32)
        wanted = slots_ref[...]
        for i, owner in enumerate(owners):
            first = (place_ref[0] * PLANE + (place_ref[1] ^ owner)) * per_shard
            for a in range(per_shard):
                at = (i * per_shard + a) * rank
                low += jnp.where(wanted == first + a, total[at : at + rank, :], 0.0)
        out_ref[...] = low

    whole = pl.BlockSpec(memory_space=pltpu.VMEM)
    held_in = [pltpu.with_memory_space_constraint(x, pltpu.VMEM) for x in (*tables, *hidden)]
    return pl.pallas_call(
        body,
        grid_spec=pltpu.PrefetchScalarGridSpec(
            num_scalar_prefetch=1,
            grid=(1,),
            in_specs=[whole] * (1 + len(held_in)),
            out_specs=whole,
            scratch_shapes=[
                pltpu.VMEM((lanes, width), BF16),
                pltpu.VMEM((count * rows, width), BF16),
            ],
        ),
        out_shape=jax.ShapeDtypeStruct((rank, lanes), F32),
        cost_estimate=cost(
            2 * lanes * count * rows * len(sources) * width,
            2 * (lanes + count * rows) * len(sources) * width,
            share,
        ),
        compiler_params=params(10),
        name="low_part",
    )(place, slots, *held_in)


def add_extra(place, low, slots, mine, other, keep, recv, first_step, pieces, per_shard, rank):
    _, planes, _, requests, width = keep.shape
    rows, lanes = mine.shape[0], low.shape[1]
    half = planes // 2
    parts = {
        KEEP_Y: ((0,), range(planes)),
        SEND_Y: ((1,), range(planes)),
        KEEP_Z: ((0, 1), range(half)),
        SEND_Z: ((0, 1), range(half, planes)),
    }

    def body(place_ref, low_ref, slots_ref, m_ref, t_ref, k_ref, r_ref, *out_refs):
        rounded = low_ref[...].astype(BF16).astype(F32)
        wanted = slots_ref[...]
        spread = []
        for i in range(2):
            first = (place_ref[0] * PLANE + (place_ref[1] ^ i)) * per_shard
            masked = [jnp.where(wanted == first + a, rounded, 0.0) for a in range(per_shard)]
            spread.append(jnp.concatenate(masked, axis=0).T.astype(BF16))
        for (step, what, part, share), out_ref in zip(pieces, out_refs):
            size = requests // share
            start = (step - first_step) * requests + part * size
            here = [value[start : start + size] for value in spread]
            rows_at = slice(part * size, (part + 1) * size)
            for side_at, side in enumerate(parts[what][0]):
                for block_at, i in enumerate(parts[what][1]):
                    block = (place_ref[0] ^ halving(i, planes)) * PLANE + (place_ref[1] ^ (2 * side))
                    columns = pl.ds(pl.multiple_of(block * width, width), width)
                    own, other_own = m_ref[:, columns], t_ref[1, i, :, side * width : (side + 1) * width]
                    extra = jnp.dot(here[0], own, preferred_element_type=F32)
                    extra += jnp.dot(here[1], other_own, preferred_element_type=F32)
                    base = k_ref[side, i, step, rows_at] + r_ref[side, i, step, rows_at].astype(F32)
                    out_ref[side_at, block_at] = (base + extra).astype(out_ref.dtype)

    def shape(step, what, part, share):
        return (len(parts[what][0]), len(parts[what][1]), requests // share, width)

    whole = pl.BlockSpec(memory_space=pltpu.VMEM)
    return pl.pallas_call(
        body,
        grid_spec=pltpu.PrefetchScalarGridSpec(
            num_scalar_prefetch=1,
            grid=(1,),
            in_specs=[whole] * 6,
            out_specs=[whole] * len(pieces),
        ),
        out_shape=[
            jax.ShapeDtypeStruct(shape(*piece), BF16 if piece[1] in (SEND_Y, SEND_Z) else F32)
            for piece in pieces
        ],
        cost_estimate=cost(4 * lanes * rows * planes * width, 10 * lanes * planes * width),
        compiler_params=params(10),
        name="add_extra",
    )(
        place,
        low,
        slots,
        *[pltpu.with_memory_space_constraint(x, pltpu.VMEM) for x in (mine, other, keep, recv)],
    )


def local(hidden, down_matrix, first_table, second_table, storage_index, request_adapter):
    steps, requests, units = hidden.shape
    per_shard, rank, all_units = first_table.shape
    features = second_table.shape[2]
    adapters = storage_index.shape[0]
    devices = all_units // units
    planes = devices // PLANE
    width = features // devices
    me = lax.axis_index("tensor").astype(jnp.int32)
    z, w = me // PLANE, me % PLANE
    place = jnp.stack([z, w, ((z == 1) | (z == 2)).astype(jnp.int32)])

    def in_plane(value, other):
        return lax.ppermute(value, "tensor", [(t, t ^ other) for t in range(devices)])

    def along(value, other):
        return lax.ppermute(value, "tensor", [(t, t ^ (other * PLANE)) for t in range(devices)])

    def hop(value, moves):
        pairs = [(a * PLANE + v, b * PLANE + v) for a, b in moves for v in range(PLANE)]
        return lax.ppermute(value, "tensor", pairs)

    table = jnp.arange(adapters, dtype=jnp.int32)
    slot_row = jnp.sum(
        jnp.where(request_adapter[:, None] == table[None, :], storage_index[None, :], 0), axis=1
    ).astype(jnp.int32)

    first = first_table.reshape(per_shard * rank, all_units)
    second = second_table.reshape(per_shard * rank, features)

    if planes == 4:
        order = jnp.stack([z, z ^ 1, jnp.where(z < 2, 2, 1), jnp.where(z < 2, 3, 0)])
    else:
        order = jnp.stack([z ^ o for o in range(planes)])
    split = planes // 2

    for_near = pack_factors(place, order, first, units, 2)
    near_y = in_plane(for_near, 2)
    hidden_z = hidden
    if planes == 4:
        near = along(hidden_z, 1)
        middle = hop(hidden_z, ((1, 2), (2, 1)))
    else:
        blocks = [hidden] + [along(hidden_z, o) for o in range(1, planes)]
        near = middle = blocks[1]
    for_far = pack_factors(place, order, after(first, for_near), units, 3)
    for_self = pack_factors(place, order, after(first, for_far), units, 0)
    for_core = pack_core(place, order, after(first, for_self), second, width)
    send, keep = base_blocks(place, after(hidden, for_core), down_matrix, planes, width)
    near, middle, send, near_y = lax.optimization_barrier((near, middle, send, near_y))
    from_core = in_plane(after(for_core, near), 1)
    far_y = in_plane(after(for_far, near_y), 3)
    recv = in_plane(send, 1)

    at_hand = [[hidden], [near]] if planes == 4 else [[block] for block in blocks[:split]]
    slots = jnp.tile(slot_row[None, :], (1, steps))

    def low_at(chunk, owners, tables, sources, first_plane):
        share = 1 if chunk[0] == 0 else 1000
        lanes = slots[:, chunk[0] * requests : chunk[1] * requests]
        return low_part(
            place, lanes, owners, tables, sources, first_plane, chunk, per_shard, rank, share
        )

    def early_of(*ready):
        near_by = (for_self, after(from_core, *ready), near_y)
        part = low_at((0, steps), (0, 1, 2), near_by, at_hand, 0)
        return part, low_at((0, steps), (3,), (after(far_y, part),), at_hand, 0)

    def late_of(chunk, plane, source, *ready):
        tables = (for_self, after(from_core, *ready), near_y, far_y)
        return low_at(chunk, range(PLANE), tables, [source], plane)

    if planes == 4:
        outward, across = ((1, 0), (2, 3)), ((1, 2), (2, 1))
        (a, b), (c, d) = LOW_CHUNKS
        outer_one = hop(middle[a:b], outward)
        middle_two = hop(near[a:b], across)
        outer_two = hop(after(middle_two, outer_one), outward)
        early, early_far = early_of(outer_one, middle_two)
        part = late_of((a, b), 2, [middle, outer_one], early_far)
        middle_two_first = middle_two
        middle_two = hop(after(near[c:d], middle_two), across)
        outer_one = hop(after(middle[c:d], outer_one), outward)
        last = late_of((a, b), 3, [middle_two_first, outer_two], part)
        outer_two = hop(after(middle_two, last), outward)
        late = [[part, last], [[middle, outer_one], [middle_two, outer_two]]]
        second_wave = [outer_one]
    else:
        early, early_far = early_of()
        late = [[[block] for block in blocks[split:]] for _ in LOW_CHUNKS]
        second_wave = []

    def core_sum(chunk, parts):
        low = (early + early_far)[:, chunk[0] * requests : chunk[1] * requests]
        for part in parts:
            low = low + part
        return low + in_plane(low, 1)

    def with_extra(low, first_step, pieces):
        lanes = slots[:, : low.shape[1]]
        return add_extra(
            place, low, lanes, second, from_core, keep, recv, first_step, pieces, per_shard, rank
        )

    along_z = [1 << bit for bit in range(planes.bit_length() - 1)]
    y_first, z_first = ["y", *along_z], [*along_z[:1], "y", *along_z[1:]]
    plans = [list(plan) for plan in (y_first, z_first, y_first, z_first, y_first)]
    state = [None] * len(plans)

    def send(value, stage):
        return in_plane(value, 2) if stage == "y" else along(value, stage)

    def add(c, *ready):
        value, received = state[c]
        total = value + after(received, *ready).astype(F32)
        plans[c].pop(0)
        if not plans[c]:
            state[c] = (total, None)
            return total
        count = total.shape[0] // 2
        stays, goes = total[:count], total[count:].astype(BF16)
        if plans[c][0] == "y":
            stays, goes = stays[0], goes[0]
        state[c] = (stays, send(goes, plans[c][0]))
        return goes

    def begin(c, stays, goes):
        if plans[c][0] == "y":
            stays, goes = stays[0], goes[0]
        state[c] = (stays, send(goes, plans[c][0]))

    parts, ready = [], early_far
    for i, source in enumerate(late[0]):
        part = late_of(LOW_CHUNKS[0], split + i, source, ready) if isinstance(source, list) else source
        parts.append(part)
        ready = part
    low = core_sum(LOW_CHUNKS[0], parts)
    low = low + in_plane(low, 2)
    (goes,) = with_extra(low[:, :requests], 0, [(0, SEND_Y, 0, 1)])
    low = after(low, goes, *second_wave)
    moved = send(goes[0], "y")
    stays, goes, next_stays = with_extra(low, 0, [(0, KEEP_Y, 0, 1), (1, SEND_Z, 0, 1), (1, KEEP_Z, 0, 1)])
    state[0] = (stays[0], moved)
    parts, ready = [], (stays, goes, next_stays)
    for i, source in enumerate(late[1]):
        source = [after(array, *ready) for array in source]
        parts.append(late_of(LOW_CHUNKS[1], split + i, source, *ready))
        ready = (parts[-1],)
    begin(1, next_stays, after(goes, parts[0]))

    low = core_sum(LOW_CHUNKS[1], parts)
    across_y = in_plane(low, 2)
    done = add(0, low)
    low = low + after(across_y, done)
    (moved,) = with_extra(low[:, :requests], 2, [(2, SEND_Y, 0, 1)])
    done = add(1, moved)
    low = after(low, done)
    sent_y = send(moved[0], "y")
    stays, goes, next_stays, last_goes, last_stays = with_extra(
        low,
        2,
        [(2, KEEP_Y, 0, 1), (3, SEND_Z, 0, 2), (3, KEEP_Z, 0, 2), (3, SEND_Y, 1, 2), (3, KEEP_Y, 1, 2)],
    )
    state[2] = (stays[0], sent_y)
    begin(3, next_stays, goes)
    begin(4, last_stays, last_goes)
    done = next_stays
    for c in (0, 2, 3, 1, 4, 0, 2, 3, 4, 1, 2, 3, 4):
        if plans[c]:
            done = add(c, done)
    for c in range(len(plans)):
        while plans[c]:
            done = add(c, done)
    outputs = [value[0].astype(BF16) for value, _ in state]
    return jnp.concatenate(outputs, axis=0).reshape(steps, requests, width)


def solution(mesh):
    in_specs = (
        P(None, "groups", "tensor"),
        P("tensor", None),
        P(("groups", "tensor"), None, None),
        P(("groups", "tensor"), None, None),
        P("groups"),
        P("groups"),
    )
    out_specs = P(None, "groups", "tensor")
    return jax.shard_map(local, mesh=mesh, in_specs=in_specs, out_specs=out_specs, check_vma=False)
```

```python
import jax
import jax.numpy as jnp
from jax import lax
from jax.experimental import pallas as pl
from jax.experimental.pallas import tpu as pltpu
from jax.sharding import PartitionSpec as P

PLANE = 4
F32 = jnp.float32
BF16 = jnp.bfloat16
LOW_CHUNKS = ((0, 2), (2, 4))
KEEP_Y, SEND_Y, KEEP_Z, SEND_Z = range(4)


def halving(i, planes):
    out, bit = 0, 1
    while bit < planes:
        out = out * 2 + ((i // bit) % 2)
        bit *= 2
    return out


def after(value, *others):
    return lax.optimization_barrier((value, *others))[0]


def cost(flops, moved, share=1000):
    return pl.CostEstimate(
        flops=int(flops) // share, bytes_accessed=int(moved) // share, transcendentals=0
    )


def hbm(*values):
    return [pltpu.with_memory_space_constraint(value, pltpu.HBM) for value in values]


def params(mebibytes):
    return pltpu.CompilerParams(vmem_limit_bytes=mebibytes * 1024 * 1024)


def pack_factors(place, order, table, width, other):
    rows = table.shape[0]
    planes = table.shape[1] // (PLANE * width)

    def body(place_ref, order_ref, *refs):
        for i in range(planes):
            refs[planes][i] = refs[i][...]

    def columns(i):
        return lambda j, p, o: (0, o[i] * PLANE + (p[1] ^ other))

    return pl.pallas_call(
        body,
        grid_spec=pltpu.PrefetchScalarGridSpec(
            num_scalar_prefetch=2,
            grid=(1,),
            in_specs=[pl.BlockSpec((rows, width), columns(i)) for i in range(planes)],
            out_specs=pl.BlockSpec((planes, rows, width), lambda i, p, o: (0, 0, 0)),
        ),
        out_shape=jax.ShapeDtypeStruct((planes, rows, width), BF16),
        cost_estimate=cost(0, 4 * planes * rows * width),
        compiler_params=params(10),
        name="pack_factors",
    )(place, order, *hbm(*([table] * planes)))


def pack_core(place, order, first, second, width):
    rows, units = first.shape[0], 2 * width
    planes = first.shape[1] // (PLANE * units)

    def body(place_ref, order_ref, a_ref, s0_ref, s1_ref, out_ref):
        out_ref[0, 0] = a_ref[...]
        out_ref[1, 0, :, :width] = s0_ref[...]
        out_ref[1, 0, :, width:] = s1_ref[...]

    def columns(side):
        return lambda i, p, o: (
            0,
            (p[0] ^ halving(i, planes)) * PLANE + (p[1] ^ 1 ^ (2 * side)),
        )

    return pl.pallas_call(
        body,
        grid_spec=pltpu.PrefetchScalarGridSpec(
            num_scalar_prefetch=2,
            grid=(planes,),
            in_specs=[pl.BlockSpec((rows, units), lambda i, p, o: (0, o[i] * PLANE + (p[1] ^ 1)))]
            + [pl.BlockSpec((rows, width), columns(side)) for side in (0, 1)],
            out_specs=pl.BlockSpec((2, 1, rows, units), lambda i, p, o: (0, i, 0, 0)),
        ),
        out_shape=jax.ShapeDtypeStruct((2, planes, rows, units), BF16),
        cost_estimate=cost(0, 8 * planes * rows * units),
        compiler_params=params(10),
        name="pack_core",
    )(place, order, *hbm(first, second, second))


def base_blocks(place, hidden, down, planes, width):
    steps, rows, units = hidden.shape

    def body(place_ref, hidden_ref, d0, d1, d2, d3, send_ref, keep_ref):
        flat = hidden_ref[...].reshape(steps * rows, units)
        for i, ref in enumerate((d0, d1, d2, d3)):
            value = jnp.dot(flat, ref[...], preferred_element_type=F32).reshape(steps, rows, width)
            if i & 1:
                send_ref[i >> 1, 0] = value.astype(BF16)
            else:
                keep_ref[i >> 1, 0] = value

    def columns(other):
        return lambda i, p: (0, (p[0] ^ halving(i, planes)) * PLANE + (p[1] ^ other))

    shape = (2, planes, steps, rows, width)
    return pl.pallas_call(
        body,
        grid_spec=pltpu.PrefetchScalarGridSpec(
            num_scalar_prefetch=1,
            grid=(planes,),
            in_specs=[pl.BlockSpec((steps, rows, units), lambda i, p: (0, 0, 0))]
            + [pl.BlockSpec((units, width), columns(o)) for o in range(PLANE)],
            out_specs=[pl.BlockSpec((2, 1, steps, rows, width), lambda i, p: (0, i, 0, 0, 0))] * 2,
        ),
        out_shape=[jax.ShapeDtypeStruct(shape, BF16), jax.ShapeDtypeStruct(shape, F32)],
        cost_estimate=cost(
            2 * steps * rows * units * down.shape[1], (2 * units + 3 * steps * rows) * down.shape[1]
        ),
        compiler_params=params(24),
        name="base_blocks",
    )(place, *hbm(hidden, down, down, down, down))


def low_part(place, slots, owners, tables, sources, first_plane, chunk, per_shard, rank, share):
    first_step, last_step = chunk
    steps = last_step - first_step
    rows, (_, requests, width) = tables[-1].shape[-2], sources[0][0].shape
    lanes, count = steps * requests, len(owners)
    hidden = [array for source in sources for array in source]

    def body(place_ref, slots_ref, *refs):
        factor_refs, hidden_refs = refs[:count], refs[count : count + len(hidden)]
        out_ref, held, factors = refs[count + len(hidden) :]
        total, at = None, 0
        for j, source in enumerate(sources):
            for inner in range(len(source)):
                ref = hidden_refs[at]
                start = first_step if ref.shape[0] > steps else 0
                if len(source) == 1:
                    held[...] = ref[start : start + steps].reshape(lanes, width)
                else:

                    @pl.when(place_ref[2] == 1 - inner)
                    def _(ref=ref, start=start):
                        held[...] = ref[start : start + steps].reshape(lanes, width)

                at += 1
            for i, ref in enumerate(factor_refs):
                factors[i * rows : (i + 1) * rows, :] = (
                    ref[0, first_plane + j] if ref.shape[0] == 2 else ref[first_plane + j]
                )
            product = lax.dot_general(
                factors[...], held[...], (((1,), (1,)), ((), ())), preferred_element_type=F32
            )
            total = product if total is None else total + product
        low = jnp.zeros((rank, lanes), F32)
        wanted = slots_ref[...]
        for i, owner in enumerate(owners):
            first = (place_ref[0] * PLANE + (place_ref[1] ^ owner)) * per_shard
            for a in range(per_shard):
                at = (i * per_shard + a) * rank
                low += jnp.where(wanted == first + a, total[at : at + rank, :], 0.0)
        out_ref[...] = low

    whole = pl.BlockSpec(memory_space=pltpu.VMEM)
    held_in = [pltpu.with_memory_space_constraint(x, pltpu.VMEM) for x in (*tables, *hidden)]
    return pl.pallas_call(
        body,
        grid_spec=pltpu.PrefetchScalarGridSpec(
            num_scalar_prefetch=1,
            grid=(1,),
            in_specs=[whole] * (1 + len(held_in)),
            out_specs=whole,
            scratch_shapes=[
                pltpu.VMEM((lanes, width), BF16),
                pltpu.VMEM((count * rows, width), BF16),
            ],
        ),
        out_shape=jax.ShapeDtypeStruct((rank, lanes), F32),
        cost_estimate=cost(
            2 * lanes * count * rows * len(sources) * width,
            2 * (lanes + count * rows) * len(sources) * width,
            share,
        ),
        compiler_params=params(10),
        name="low_part",
    )(place, slots, *held_in)


def add_extra(place, low, slots, mine, other, keep, recv, first_row, pieces, per_shard, rank):
    _, planes, _, width = keep.shape
    rows, lanes = mine.shape[0], low.shape[1]
    half = planes // 2
    parts = {
        KEEP_Y: ((0,), range(planes)),
        SEND_Y: ((1,), range(planes)),
        KEEP_Z: ((0, 1), range(half)),
        SEND_Z: ((0, 1), range(half, planes)),
    }

    def body(place_ref, low_ref, slots_ref, m_ref, t_ref, k_ref, r_ref, *out_refs):
        rounded = low_ref[...].astype(BF16).astype(F32)
        wanted = slots_ref[...]
        spread = []
        for i in range(2):
            first = (place_ref[0] * PLANE + (place_ref[1] ^ i)) * per_shard
            masked = [jnp.where(wanted == first + a, rounded, 0.0) for a in range(per_shard)]
            spread.append(jnp.concatenate(masked, axis=0).T.astype(BF16))
        for (what, row, size), out_ref in zip(pieces, out_refs):
            start = row - first_row
            here = [value[start : start + size] for value in spread]
            rows_at = slice(row, row + size)
            for side_at, side in enumerate(parts[what][0]):
                for block_at, i in enumerate(parts[what][1]):
                    block = (place_ref[0] ^ halving(i, planes)) * PLANE + (place_ref[1] ^ (2 * side))
                    columns = pl.ds(pl.multiple_of(block * width, width), width)
                    own, other_own = m_ref[:, columns], t_ref[1, i, :, side * width : (side + 1) * width]
                    extra = jnp.dot(here[0], own, preferred_element_type=F32)
                    extra += jnp.dot(here[1], other_own, preferred_element_type=F32)
                    base = k_ref[side, i, rows_at] + r_ref[side, i, rows_at].astype(F32)
                    out_ref[side_at, block_at] = (base + extra).astype(out_ref.dtype)

    def shape(what, row, size):
        return (len(parts[what][0]), len(parts[what][1]), size, width)

    whole = pl.BlockSpec(memory_space=pltpu.VMEM)
    return pl.pallas_call(
        body,
        grid_spec=pltpu.PrefetchScalarGridSpec(
            num_scalar_prefetch=1,
            grid=(1,),
            in_specs=[whole] * 6,
            out_specs=[whole] * len(pieces),
        ),
        out_shape=[
            jax.ShapeDtypeStruct(shape(*piece), BF16 if piece[0] in (SEND_Y, SEND_Z) else F32)
            for piece in pieces
        ],
        cost_estimate=cost(4 * lanes * rows * planes * width, 10 * lanes * planes * width),
        compiler_params=params(10),
        name="add_extra",
    )(
        place,
        low,
        slots,
        *[pltpu.with_memory_space_constraint(x, pltpu.VMEM) for x in (mine, other, keep, recv)],
    )


def local(hidden, down_matrix, first_table, second_table, storage_index, request_adapter):
    steps, requests, units = hidden.shape
    per_shard, rank, all_units = first_table.shape
    features = second_table.shape[2]
    adapters = storage_index.shape[0]
    devices = all_units // units
    planes = devices // PLANE
    width = features // devices
    me = lax.axis_index("tensor").astype(jnp.int32)
    z, w = me // PLANE, me % PLANE
    place = jnp.stack([z, w, ((z == 1) | (z == 2)).astype(jnp.int32)])

    def in_plane(value, other):
        return lax.ppermute(value, "tensor", [(t, t ^ other) for t in range(devices)])

    def along(value, other):
        return lax.ppermute(value, "tensor", [(t, t ^ (other * PLANE)) for t in range(devices)])

    def hop(value, moves):
        pairs = [(a * PLANE + v, b * PLANE + v) for a, b in moves for v in range(PLANE)]
        return lax.ppermute(value, "tensor", pairs)

    table = jnp.arange(adapters, dtype=jnp.int32)
    slot_row = jnp.sum(
        jnp.where(request_adapter[:, None] == table[None, :], storage_index[None, :], 0), axis=1
    ).astype(jnp.int32)

    first = first_table.reshape(per_shard * rank, all_units)
    second = second_table.reshape(per_shard * rank, features)

    if planes == 4:
        order = jnp.stack([z, z ^ 1, jnp.where(z < 2, 2, 1), jnp.where(z < 2, 3, 0)])
    else:
        order = jnp.stack([z ^ o for o in range(planes)])
    split = planes // 2

    for_near = pack_factors(place, order, first, units, 2)
    near_y = in_plane(for_near, 2)
    hidden_z = hidden
    if planes == 4:
        near = along(hidden_z, 1)
        middle = hop(hidden_z, ((1, 2), (2, 1)))
    else:
        blocks = [hidden] + [along(hidden_z, o) for o in range(1, planes)]
        near = middle = blocks[1]
    for_far = pack_factors(place, order, after(first, for_near), units, 3)
    for_self = pack_factors(place, order, after(first, for_far), units, 0)
    for_core = pack_core(place, order, after(first, for_self), second, width)
    send, keep = base_blocks(place, after(hidden, for_core), down_matrix, planes, width)
    near, middle, send, near_y = lax.optimization_barrier((near, middle, send, near_y))
    from_core = in_plane(after(for_core, near), 1)
    far_y = in_plane(after(for_far, near_y), 3)
    recv = in_plane(send, 1)

    at_hand = [[hidden], [near]] if planes == 4 else [[block] for block in blocks[:split]]
    slots = jnp.tile(slot_row[None, :], (1, steps))

    def low_at(chunk, owners, tables, sources, first_plane):
        share = 1 if chunk[0] == 0 else 1000
        lanes = slots[:, chunk[0] * requests : chunk[1] * requests]
        return low_part(
            place, lanes, owners, tables, sources, first_plane, chunk, per_shard, rank, share
        )

    def early_of(*ready):
        near_by = (for_self, after(from_core, *ready), near_y)
        part = low_at((0, steps), (0, 1, 2), near_by, at_hand, 0)
        return part, low_at((0, steps), (3,), (after(far_y, part),), at_hand, 0)

    def late_of(chunk, plane, source, *ready):
        tables = (for_self, after(from_core, *ready), near_y, far_y)
        return low_at(chunk, range(PLANE), tables, [source], plane)

    if planes == 4:
        outward, across = ((1, 0), (2, 3)), ((1, 2), (2, 1))
        (a, b), (c, d) = LOW_CHUNKS
        outer_one = hop(middle[a:b], outward)
        middle_two = hop(near[a:b], across)
        outer_two = hop(after(middle_two, outer_one), outward)
        early, early_far = early_of(outer_one, middle_two)
        part = late_of((a, b), 2, [middle, outer_one], early_far)
        middle_two_first = middle_two
        middle_two = hop(after(near[c:d], middle_two), across)
        outer_one = hop(after(middle[c:d], outer_one), outward)
        last = late_of((a, b), 3, [middle_two_first, outer_two], part)
        outer_two = hop(after(middle_two, last), outward)
        late = [[part, last], [[middle, outer_one], [middle_two, outer_two]]]
        second_wave = [outer_one]
    else:
        early, early_far = early_of()
        late = [[[block] for block in blocks[split:]] for _ in LOW_CHUNKS]
        second_wave = []

    def core_sum(chunk, parts):
        low = (early + early_far)[:, chunk[0] * requests : chunk[1] * requests]
        for part in parts:
            low = low + part
        return low + in_plane(low, 1)

    flat = (2, planes, steps * requests, width)
    keep, recv = keep.reshape(flat), recv.reshape(flat)

    def with_extra(low, first_row, pieces):
        lanes = slots[:, : low.shape[1]]
        return add_extra(
            place, low, lanes, second, from_core, keep, recv, first_row, pieces, per_shard, rank
        )

    along_z = [1 << bit for bit in range(planes.bit_length() - 1)]
    y_first, z_first = ["y", *along_z], [*along_z[:1], "y", *along_z[1:]]
    plans = [list(plan) for plan in (y_first, z_first, y_first, z_first, y_first)]
    state = [None] * len(plans)

    def send(value, stage):
        return in_plane(value, 2) if stage == "y" else along(value, stage)

    def add(c, *ready):
        value, received = state[c]
        total = value + after(received, *ready).astype(F32)
        plans[c].pop(0)
        if not plans[c]:
            state[c] = (total, None)
            return total
        count = total.shape[0] // 2
        stays, goes = total[:count], total[count:].astype(BF16)
        if plans[c][0] == "y":
            stays, goes = stays[0], goes[0]
        state[c] = (stays, send(goes, plans[c][0]))
        return goes

    def begin(c, stays, goes):
        if plans[c][0] == "y":
            stays, goes = stays[0], goes[0]
        state[c] = (stays, send(goes, plans[c][0]))

    parts, ready = [], early_far
    for i, source in enumerate(late[0]):
        part = late_of(LOW_CHUNKS[0], split + i, source, ready) if isinstance(source, list) else source
        parts.append(part)
        ready = part
    low = core_sum(LOW_CHUNKS[0], parts)
    low = low + in_plane(low, 2)
    half = requests // 2
    rows = [0, requests + half // 2, 2 * requests, 3 * requests, 3 * requests + half, steps * requests]
    spans = [(a, b - a) for a, b in zip(rows, rows[1:])]
    (goes,) = with_extra(low, 0, [(SEND_Y, *spans[0])])
    low = after(low, goes, *second_wave)
    moved = send(goes[0], "y")
    stays, goes, next_stays = with_extra(
        low, 0, [(KEEP_Y, *spans[0]), (SEND_Z, *spans[1]), (KEEP_Z, *spans[1])]
    )
    state[0] = (stays[0], moved)
    parts, ready = [], (stays, goes, next_stays)
    for i, source in enumerate(late[1]):
        source = [after(array, *ready) for array in source]
        parts.append(late_of(LOW_CHUNKS[1], split + i, source, *ready))
        ready = (parts[-1],)
    begin(1, next_stays, after(goes, parts[0]))

    low = core_sum(LOW_CHUNKS[1], parts)
    across_y = in_plane(low, 2)
    done = add(0, low)
    low = low + after(across_y, done)
    (moved,) = with_extra(low, spans[2][0], [(SEND_Y, *spans[2])])
    done = add(1, moved)
    low = after(low, done)
    sent_y = send(moved[0], "y")
    stays, goes, next_stays, last_goes, last_stays = with_extra(
        low,
        spans[2][0],
        [
            (KEEP_Y, *spans[2]),
            (SEND_Z, *spans[3]),
            (KEEP_Z, *spans[3]),
            (SEND_Y, *spans[4]),
            (KEEP_Y, *spans[4]),
        ],
    )
    state[2] = (stays[0], sent_y)
    begin(3, next_stays, goes)
    begin(4, last_stays, last_goes)
    done = next_stays
    for c in (0, 2, 1, 3, 4, 2, 3, 4, 0, 1, 2, 3, 4):
        if plans[c]:
            done = add(c, done)
    for c in range(len(plans)):
        while plans[c]:
            done = add(c, done)
    outputs = [value[0].astype(BF16) for value, _ in state]
    return jnp.concatenate(outputs, axis=0).reshape(steps, requests, width)


def solution(mesh):
    in_specs = (
        P(None, "groups", "tensor"),
        P("tensor", None),
        P(("groups", "tensor"), None, None),
        P(("groups", "tensor"), None, None),
        P("groups"),
        P("groups"),
    )
    out_specs = P(None, "groups", "tensor")
    return jax.shard_map(local, mesh=mesh, in_specs=in_specs, out_specs=out_specs, check_vma=False)
```

```python
import jax
import jax.numpy as jnp
from jax import lax
from jax.experimental import pallas as pl
from jax.experimental.pallas import tpu as pltpu
from jax.sharding import PartitionSpec as P

PLANE = 4
F32 = jnp.float32
BF16 = jnp.bfloat16
LOW_CHUNKS = ((0, 2), (2, 4))
KEEP_Y, SEND_Y, KEEP_Z, SEND_Z = range(4)


def halving(i, planes):
    out, bit = 0, 1
    while bit < planes:
        out = out * 2 + ((i // bit) % 2)
        bit *= 2
    return out


def after(value, *others):
    return lax.optimization_barrier((value, *others))[0]


def cost(flops, moved, share=1000):
    return pl.CostEstimate(
        flops=int(flops) // share, bytes_accessed=int(moved) // share, transcendentals=0
    )


def hbm(*values):
    return [pltpu.with_memory_space_constraint(value, pltpu.HBM) for value in values]


def params(mebibytes):
    return pltpu.CompilerParams(vmem_limit_bytes=mebibytes * 1024 * 1024)


def pack_factors(place, order, table, width, other):
    rows = table.shape[0]
    planes = table.shape[1] // (PLANE * width)

    def body(place_ref, order_ref, *refs):
        for i in range(planes):
            refs[planes][i] = refs[i][...]

    def columns(i):
        return lambda j, p, o: (0, o[i] * PLANE + (p[1] ^ other))

    return pl.pallas_call(
        body,
        grid_spec=pltpu.PrefetchScalarGridSpec(
            num_scalar_prefetch=2,
            grid=(1,),
            in_specs=[pl.BlockSpec((rows, width), columns(i)) for i in range(planes)],
            out_specs=pl.BlockSpec((planes, rows, width), lambda i, p, o: (0, 0, 0)),
        ),
        out_shape=jax.ShapeDtypeStruct((planes, rows, width), BF16),
        cost_estimate=cost(0, 4 * planes * rows * width),
        compiler_params=params(10),
        name="pack_factors",
    )(place, order, *hbm(*([table] * planes)))


def pack_core(place, order, first, second, width):
    rows, units = first.shape[0], 2 * width
    planes = first.shape[1] // (PLANE * units)

    def body(place_ref, order_ref, a_ref, s0_ref, s1_ref, out_ref):
        out_ref[0, 0] = a_ref[...]
        out_ref[1, 0, :, :width] = s0_ref[...]
        out_ref[1, 0, :, width:] = s1_ref[...]

    def columns(side):
        return lambda i, p, o: (
            0,
            (p[0] ^ halving(i, planes)) * PLANE + (p[1] ^ 1 ^ (2 * side)),
        )

    return pl.pallas_call(
        body,
        grid_spec=pltpu.PrefetchScalarGridSpec(
            num_scalar_prefetch=2,
            grid=(planes,),
            in_specs=[pl.BlockSpec((rows, units), lambda i, p, o: (0, o[i] * PLANE + (p[1] ^ 1)))]
            + [pl.BlockSpec((rows, width), columns(side)) for side in (0, 1)],
            out_specs=pl.BlockSpec((2, 1, rows, units), lambda i, p, o: (0, i, 0, 0)),
        ),
        out_shape=jax.ShapeDtypeStruct((2, planes, rows, units), BF16),
        cost_estimate=cost(0, 8 * planes * rows * units),
        compiler_params=params(10),
        name="pack_core",
    )(place, order, *hbm(first, second, second))


def base_blocks(place, hidden, down, planes, width):
    steps, rows, units = hidden.shape

    def body(place_ref, hidden_ref, d0, d1, d2, d3, send_ref, keep_ref):
        flat = hidden_ref[...].reshape(steps * rows, units)
        for i, ref in enumerate((d0, d1, d2, d3)):
            value = jnp.dot(flat, ref[...], preferred_element_type=F32).reshape(steps, rows, width)
            if i & 1:
                send_ref[i >> 1, 0] = value.astype(BF16)
            else:
                keep_ref[i >> 1, 0] = value

    def columns(other):
        return lambda i, p: (0, (p[0] ^ halving(i, planes)) * PLANE + (p[1] ^ other))

    shape = (2, planes, steps, rows, width)
    return pl.pallas_call(
        body,
        grid_spec=pltpu.PrefetchScalarGridSpec(
            num_scalar_prefetch=1,
            grid=(planes,),
            in_specs=[pl.BlockSpec((steps, rows, units), lambda i, p: (0, 0, 0))]
            + [pl.BlockSpec((units, width), columns(o)) for o in range(PLANE)],
            out_specs=[pl.BlockSpec((2, 1, steps, rows, width), lambda i, p: (0, i, 0, 0, 0))] * 2,
        ),
        out_shape=[jax.ShapeDtypeStruct(shape, BF16), jax.ShapeDtypeStruct(shape, F32)],
        cost_estimate=cost(
            2 * steps * rows * units * down.shape[1], (2 * units + 3 * steps * rows) * down.shape[1]
        ),
        compiler_params=params(24),
        name="base_blocks",
    )(place, *hbm(hidden, down, down, down, down))


def low_part(place, slots, owners, tables, sources, first_plane, chunk, per_shard, rank, share):
    first_step, last_step = chunk
    steps = last_step - first_step
    rows, (_, requests, width) = tables[-1].shape[-2], sources[0][0].shape
    lanes, count = steps * requests, len(owners)
    hidden = [array for source in sources for array in source]

    def body(place_ref, slots_ref, *refs):
        factor_refs, hidden_refs = refs[:count], refs[count : count + len(hidden)]
        out_ref, held, factors = refs[count + len(hidden) :]
        total, at = None, 0
        for j, source in enumerate(sources):
            for inner in range(len(source)):
                ref = hidden_refs[at]
                start = first_step if ref.shape[0] > steps else 0
                if len(source) == 1:
                    held[...] = ref[start : start + steps].reshape(lanes, width)
                else:

                    @pl.when(place_ref[2] == 1 - inner)
                    def _(ref=ref, start=start):
                        held[...] = ref[start : start + steps].reshape(lanes, width)

                at += 1
            for i, ref in enumerate(factor_refs):
                factors[i * rows : (i + 1) * rows, :] = (
                    ref[0, first_plane + j] if ref.shape[0] == 2 else ref[first_plane + j]
                )
            product = lax.dot_general(
                factors[...], held[...], (((1,), (1,)), ((), ())), preferred_element_type=F32
            )
            total = product if total is None else total + product
        low = jnp.zeros((rank, lanes), F32)
        wanted = slots_ref[...]
        for i, owner in enumerate(owners):
            first = (place_ref[0] * PLANE + (place_ref[1] ^ owner)) * per_shard
            for a in range(per_shard):
                at = (i * per_shard + a) * rank
                low += jnp.where(wanted == first + a, total[at : at + rank, :], 0.0)
        out_ref[...] = low

    whole = pl.BlockSpec(memory_space=pltpu.VMEM)
    held_in = [pltpu.with_memory_space_constraint(x, pltpu.VMEM) for x in (*tables, *hidden)]
    return pl.pallas_call(
        body,
        grid_spec=pltpu.PrefetchScalarGridSpec(
            num_scalar_prefetch=1,
            grid=(1,),
            in_specs=[whole] * (1 + len(held_in)),
            out_specs=whole,
            scratch_shapes=[
                pltpu.VMEM((lanes, width), BF16),
                pltpu.VMEM((count * rows, width), BF16),
            ],
        ),
        out_shape=jax.ShapeDtypeStruct((rank, lanes), F32),
        cost_estimate=cost(
            2 * lanes * count * rows * len(sources) * width,
            2 * (lanes + count * rows) * len(sources) * width,
            share,
        ),
        compiler_params=params(10),
        name="low_part",
    )(place, slots, *held_in)


def add_extra(place, low, slots, mine, other, keep, recv, first_row, pieces, per_shard, rank):
    _, planes, _, width = keep.shape
    rows, lanes = mine.shape[0], low.shape[1]
    half = planes // 2
    parts = {
        KEEP_Y: ((0,), range(planes)),
        SEND_Y: ((1,), range(planes)),
        KEEP_Z: ((0, 1), range(half)),
        SEND_Z: ((0, 1), range(half, planes)),
    }

    def body(place_ref, low_ref, slots_ref, m_ref, t_ref, k_ref, r_ref, *out_refs):
        rounded = low_ref[...].astype(BF16).astype(F32)
        wanted = slots_ref[...]
        spread = []
        for i in range(2):
            first = (place_ref[0] * PLANE + (place_ref[1] ^ i)) * per_shard
            masked = [jnp.where(wanted == first + a, rounded, 0.0) for a in range(per_shard)]
            spread.append(jnp.concatenate(masked, axis=0).T.astype(BF16))
        for (what, row, size), out_ref in zip(pieces, out_refs):
            start = row - first_row
            here = [value[start : start + size] for value in spread]
            rows_at = slice(row, row + size)
            for side_at, side in enumerate(parts[what][0]):
                for block_at, i in enumerate(parts[what][1]):
                    block = (place_ref[0] ^ halving(i, planes)) * PLANE + (place_ref[1] ^ (2 * side))
                    columns = pl.ds(pl.multiple_of(block * width, width), width)
                    own, other_own = m_ref[:, columns], t_ref[1, i, :, side * width : (side + 1) * width]
                    extra = jnp.dot(here[0], own, preferred_element_type=F32)
                    extra += jnp.dot(here[1], other_own, preferred_element_type=F32)
                    base = k_ref[side, i, rows_at] + r_ref[side, i, rows_at].astype(F32)
                    out_ref[side_at, block_at] = (base + extra).astype(out_ref.dtype)

    def shape(what, row, size):
        return (len(parts[what][0]), len(parts[what][1]), size, width)

    whole = pl.BlockSpec(memory_space=pltpu.VMEM)
    return pl.pallas_call(
        body,
        grid_spec=pltpu.PrefetchScalarGridSpec(
            num_scalar_prefetch=1,
            grid=(1,),
            in_specs=[whole] * 6,
            out_specs=[whole] * len(pieces),
        ),
        out_shape=[
            jax.ShapeDtypeStruct(shape(*piece), BF16 if piece[0] in (SEND_Y, SEND_Z) else F32)
            for piece in pieces
        ],
        cost_estimate=cost(4 * lanes * rows * planes * width, 10 * lanes * planes * width, 1),
        compiler_params=params(10),
        name="add_extra",
    )(
        place,
        low,
        slots,
        *[pltpu.with_memory_space_constraint(x, pltpu.VMEM) for x in (mine, other, keep, recv)],
    )


def local(hidden, down_matrix, first_table, second_table, storage_index, request_adapter):
    steps, requests, units = hidden.shape
    per_shard, rank, all_units = first_table.shape
    features = second_table.shape[2]
    adapters = storage_index.shape[0]
    devices = all_units // units
    planes = devices // PLANE
    width = features // devices
    me = lax.axis_index("tensor").astype(jnp.int32)
    z, w = me // PLANE, me % PLANE
    place = jnp.stack([z, w, ((z == 1) | (z == 2)).astype(jnp.int32)])

    def in_plane(value, other):
        return lax.ppermute(value, "tensor", [(t, t ^ other) for t in range(devices)])

    def along(value, other):
        return lax.ppermute(value, "tensor", [(t, t ^ (other * PLANE)) for t in range(devices)])

    def hop(value, moves):
        pairs = [(a * PLANE + v, b * PLANE + v) for a, b in moves for v in range(PLANE)]
        return lax.ppermute(value, "tensor", pairs)

    table = jnp.arange(adapters, dtype=jnp.int32)
    slot_row = jnp.sum(
        jnp.where(request_adapter[:, None] == table[None, :], storage_index[None, :], 0), axis=1
    ).astype(jnp.int32)

    first = first_table.reshape(per_shard * rank, all_units)
    second = second_table.reshape(per_shard * rank, features)

    if planes == 4:
        order = jnp.stack([z, z ^ 1, jnp.where(z < 2, 2, 1), jnp.where(z < 2, 3, 0)])
    else:
        order = jnp.stack([z ^ o for o in range(planes)])
    split = planes // 2

    for_near = pack_factors(place, order, first, units, 2)
    near_y = in_plane(for_near, 2)
    hidden_z = hidden
    if planes == 4:
        near = along(hidden_z, 1)
        middle = hop(hidden_z, ((1, 2), (2, 1)))
    else:
        blocks = [hidden] + [along(hidden_z, o) for o in range(1, planes)]
        near = middle = blocks[1]
    for_far = pack_factors(place, order, after(first, for_near), units, 3)
    for_self = pack_factors(place, order, after(first, for_far), units, 0)
    for_core = pack_core(place, order, after(first, for_self), second, width)
    send, keep = base_blocks(place, after(hidden, for_core), down_matrix, planes, width)
    near, middle, send, near_y = lax.optimization_barrier((near, middle, send, near_y))
    from_core = in_plane(after(for_core, near), 1)
    far_y = in_plane(after(for_far, near_y), 3)
    recv = in_plane(send, 1)

    at_hand = [[hidden], [near]] if planes == 4 else [[block] for block in blocks[:split]]
    slots = jnp.tile(slot_row[None, :], (1, steps))

    def low_at(chunk, owners, tables, sources, first_plane):
        share = 1 if chunk[0] == 0 else 1000
        lanes = slots[:, chunk[0] * requests : chunk[1] * requests]
        return low_part(
            place, lanes, owners, tables, sources, first_plane, chunk, per_shard, rank, share
        )

    def early_of(*ready):
        near_by = (for_self, after(from_core, *ready), near_y)
        part = low_at((0, steps), (0, 1, 2), near_by, at_hand, 0)
        return part, low_at((0, steps), (3,), (after(far_y, part),), at_hand, 0)

    def late_of(chunk, plane, source, *ready):
        tables = (for_self, after(from_core, *ready), near_y, far_y)
        return low_at(chunk, range(PLANE), tables, [source], plane)

    if planes == 4:
        outward, across = ((1, 0), (2, 3)), ((1, 2), (2, 1))
        (a, b), (c, d) = LOW_CHUNKS
        outer_one = hop(middle[a:b], outward)
        middle_two = hop(near[a:b], across)
        outer_two = hop(after(middle_two, outer_one), outward)
        early, early_far = early_of(outer_one, middle_two)
        part = late_of((a, b), 2, [middle, outer_one], early_far)
        middle_two_first = middle_two
        middle_two = hop(after(near[c:d], middle_two), across)
        outer_one = hop(after(middle[c:d], outer_one), outward)
        last = late_of((a, b), 3, [middle_two_first, outer_two], part)
        outer_two = hop(after(middle_two, last), outward)
        late = [[part, last], [[middle, outer_one], [middle_two, outer_two]]]
        second_wave = [outer_one]
    else:
        early, early_far = early_of()
        late = [[[block] for block in blocks[split:]] for _ in LOW_CHUNKS]
        second_wave = []

    def core_sum(chunk, parts):
        low = (early + early_far)[:, chunk[0] * requests : chunk[1] * requests]
        for part in parts:
            low = low + part
        return low + in_plane(low, 1)

    flat = (2, planes, steps * requests, width)
    keep, recv = keep.reshape(flat), recv.reshape(flat)

    def with_extra(low, first_row, pieces):
        lanes = slots[:, : low.shape[1]]
        return add_extra(
            place, low, lanes, second, from_core, keep, recv, first_row, pieces, per_shard, rank
        )

    along_z = [1 << bit for bit in range(planes.bit_length() - 1)]
    y_first, z_first = ["y", *along_z], [*along_z[:1], "y", *along_z[1:]]
    plans = [list(plan) for plan in (y_first, z_first, y_first, z_first, y_first)]
    state = [None] * len(plans)

    def send(value, stage):
        return in_plane(value, 2) if stage == "y" else along(value, stage)

    def add(c, *ready):
        value, received = state[c]
        total = value + after(received, *ready).astype(F32)
        plans[c].pop(0)
        if not plans[c]:
            state[c] = (total, None)
            return total
        count = total.shape[0] // 2
        stays, goes = total[:count], total[count:].astype(BF16)
        if plans[c][0] == "y":
            stays, goes = stays[0], goes[0]
        state[c] = (stays, send(goes, plans[c][0]))
        return goes

    def begin(c, stays, goes):
        if plans[c][0] == "y":
            stays, goes = stays[0], goes[0]
        state[c] = (stays, send(goes, plans[c][0]))

    parts, ready = [], early_far
    for i, source in enumerate(late[0]):
        part = late_of(LOW_CHUNKS[0], split + i, source, ready) if isinstance(source, list) else source
        parts.append(part)
        ready = part
    low = core_sum(LOW_CHUNKS[0], parts)
    low = low + in_plane(low, 2)
    half = requests // 2
    rows = [0, requests + half // 2, 2 * requests, 3 * requests, 3 * requests + half, steps * requests]
    spans = [(a, b - a) for a, b in zip(rows, rows[1:])]
    (goes,) = with_extra(low, 0, [(SEND_Y, *spans[0])])
    low = after(low, goes, *second_wave)
    moved = send(goes[0], "y")
    stays, goes, next_stays = with_extra(
        low, 0, [(KEEP_Y, *spans[0]), (SEND_Z, *spans[1]), (KEEP_Z, *spans[1])]
    )
    state[0] = (stays[0], moved)
    parts, ready = [], (stays, goes, next_stays)
    for i, source in enumerate(late[1]):
        source = [after(array, *ready) for array in source]
        parts.append(late_of(LOW_CHUNKS[1], split + i, source, *ready))
        ready = (parts[-1],)
    begin(1, next_stays, after(goes, parts[0]))

    low = core_sum(LOW_CHUNKS[1], parts)
    across_y = in_plane(low, 2)
    done = add(0, low)
    low = low + after(across_y, done)
    (moved,) = with_extra(low, spans[2][0], [(SEND_Y, *spans[2])])
    done = add(1, moved)
    low = after(low, done)
    sent_y = send(moved[0], "y")
    stays, goes, next_stays, last_goes, last_stays = with_extra(
        low,
        spans[2][0],
        [
            (KEEP_Y, *spans[2]),
            (SEND_Z, *spans[3]),
            (KEEP_Z, *spans[3]),
            (SEND_Y, *spans[4]),
            (KEEP_Y, *spans[4]),
        ],
    )
    state[2] = (stays[0], sent_y)
    begin(3, next_stays, goes)
    begin(4, last_stays, last_goes)
    done = next_stays
    for c in (0, 2, 1, 3, 4, 2, 3, 4, 0, 1, 2, 3, 4):
        if plans[c]:
            done = add(c, done)
    for c in range(len(plans)):
        while plans[c]:
            done = add(c, done)
    outputs = [value[0].astype(BF16) for value, _ in state]
    return jnp.concatenate(outputs, axis=0).reshape(steps, requests, width)


def solution(mesh):
    in_specs = (
        P(None, "groups", "tensor"),
        P("tensor", None),
        P(("groups", "tensor"), None, None),
        P(("groups", "tensor"), None, None),
        P("groups"),
        P("groups"),
    )
    out_specs = P(None, "groups", "tensor")
    return jax.shard_map(local, mesh=mesh, in_specs=in_specs, out_specs=out_specs, check_vma=False)
```

```python
import jax
import jax.numpy as jnp
from jax import lax
from jax.experimental import pallas as pl
from jax.experimental.pallas import tpu as pltpu
from jax.sharding import PartitionSpec as P

PLANE = 4
F32 = jnp.float32
BF16 = jnp.bfloat16
LOW_CHUNKS = ((0, 2), (2, 4))
KEEP_Y, SEND_Y, KEEP_Z, SEND_Z = range(4)


def halving(i, planes):
    out, bit = 0, 1
    while bit < planes:
        out = out * 2 + ((i // bit) % 2)
        bit *= 2
    return out


def after(value, *others):
    return lax.optimization_barrier((value, *others))[0]


def cost(flops, moved, share=1000):
    return pl.CostEstimate(
        flops=int(flops) // share, bytes_accessed=int(moved) // share, transcendentals=0
    )


def hbm(*values):
    return [pltpu.with_memory_space_constraint(value, pltpu.HBM) for value in values]


def params(mebibytes):
    return pltpu.CompilerParams(vmem_limit_bytes=mebibytes * 1024 * 1024)


def pack_factors(place, order, table, width, other):
    rows = table.shape[0]
    planes = table.shape[1] // (PLANE * width)

    def body(place_ref, order_ref, *refs):
        for i in range(planes):
            refs[planes][i] = refs[i][...]

    def columns(i):
        return lambda j, p, o: (0, o[i] * PLANE + (p[1] ^ other))

    return pl.pallas_call(
        body,
        grid_spec=pltpu.PrefetchScalarGridSpec(
            num_scalar_prefetch=2,
            grid=(1,),
            in_specs=[pl.BlockSpec((rows, width), columns(i)) for i in range(planes)],
            out_specs=pl.BlockSpec((planes, rows, width), lambda i, p, o: (0, 0, 0)),
        ),
        out_shape=jax.ShapeDtypeStruct((planes, rows, width), BF16),
        cost_estimate=cost(0, 4 * planes * rows * width),
        compiler_params=params(10),
        name="pack_factors",
    )(place, order, *hbm(*([table] * planes)))


def pack_core(place, order, first, second, width):
    rows, units = first.shape[0], 2 * width
    planes = first.shape[1] // (PLANE * units)

    def body(place_ref, order_ref, a_ref, s0_ref, s1_ref, out_ref):
        out_ref[0, 0] = a_ref[...]
        out_ref[1, 0, :, :width] = s0_ref[...]
        out_ref[1, 0, :, width:] = s1_ref[...]

    def columns(side):
        return lambda i, p, o: (
            0,
            (p[0] ^ halving(i, planes)) * PLANE + (p[1] ^ 1 ^ (2 * side)),
        )

    return pl.pallas_call(
        body,
        grid_spec=pltpu.PrefetchScalarGridSpec(
            num_scalar_prefetch=2,
            grid=(planes,),
            in_specs=[pl.BlockSpec((rows, units), lambda i, p, o: (0, o[i] * PLANE + (p[1] ^ 1)))]
            + [pl.BlockSpec((rows, width), columns(side)) for side in (0, 1)],
            out_specs=pl.BlockSpec((2, 1, rows, units), lambda i, p, o: (0, i, 0, 0)),
        ),
        out_shape=jax.ShapeDtypeStruct((2, planes, rows, units), BF16),
        cost_estimate=cost(0, 8 * planes * rows * units),
        compiler_params=params(10),
        name="pack_core",
    )(place, order, *hbm(first, second, second))


def base_blocks(place, hidden, down, planes, width):
    steps, rows, units = hidden.shape

    def body(place_ref, hidden_ref, d0, d1, d2, d3, send_ref, keep_ref):
        flat = hidden_ref[...].reshape(steps * rows, units)
        for i, ref in enumerate((d0, d1, d2, d3)):
            value = jnp.dot(flat, ref[...], preferred_element_type=F32).reshape(steps, rows, width)
            if i & 1:
                send_ref[i >> 1, 0] = value.astype(BF16)
            else:
                keep_ref[i >> 1, 0] = value

    def columns(other):
        return lambda i, p: (0, (p[0] ^ halving(i, planes)) * PLANE + (p[1] ^ other))

    shape = (2, planes, steps, rows, width)
    return pl.pallas_call(
        body,
        grid_spec=pltpu.PrefetchScalarGridSpec(
            num_scalar_prefetch=1,
            grid=(planes,),
            in_specs=[pl.BlockSpec((steps, rows, units), lambda i, p: (0, 0, 0))]
            + [pl.BlockSpec((units, width), columns(o)) for o in range(PLANE)],
            out_specs=[pl.BlockSpec((2, 1, steps, rows, width), lambda i, p: (0, i, 0, 0, 0))] * 2,
        ),
        out_shape=[jax.ShapeDtypeStruct(shape, BF16), jax.ShapeDtypeStruct(shape, F32)],
        cost_estimate=cost(
            2 * steps * rows * units * down.shape[1], (2 * units + 3 * steps * rows) * down.shape[1]
        ),
        compiler_params=params(24),
        name="base_blocks",
    )(place, *hbm(hidden, down, down, down, down))


def low_part(place, slots, owners, tables, sources, first_plane, chunk, per_shard, rank, share):
    first_step, last_step = chunk
    steps = last_step - first_step
    rows, (_, requests, width) = tables[-1].shape[-2], sources[0][0].shape
    lanes, count = steps * requests, len(owners)
    hidden = [array for source in sources for array in source]

    def body(place_ref, slots_ref, *refs):
        factor_refs, hidden_refs = refs[:count], refs[count : count + len(hidden)]
        out_ref, held, factors = refs[count + len(hidden) :]
        total, at = None, 0
        for j, source in enumerate(sources):
            for inner in range(len(source)):
                ref = hidden_refs[at]
                start = first_step if ref.shape[0] > steps else 0
                if len(source) == 1:
                    held[...] = ref[start : start + steps].reshape(lanes, width)
                else:

                    @pl.when(place_ref[2] == 1 - inner)
                    def _(ref=ref, start=start):
                        held[...] = ref[start : start + steps].reshape(lanes, width)

                at += 1
            for i, ref in enumerate(factor_refs):
                factors[i * rows : (i + 1) * rows, :] = (
                    ref[0, first_plane + j] if ref.shape[0] == 2 else ref[first_plane + j]
                )
            product = lax.dot_general(
                factors[...], held[...], (((1,), (1,)), ((), ())), preferred_element_type=F32
            )
            total = product if total is None else total + product
        low = jnp.zeros((rank, lanes), F32)
        wanted = slots_ref[...]
        for i, owner in enumerate(owners):
            first = (place_ref[0] * PLANE + (place_ref[1] ^ owner)) * per_shard
            for a in range(per_shard):
                at = (i * per_shard + a) * rank
                low += jnp.where(wanted == first + a, total[at : at + rank, :], 0.0)
        out_ref[...] = low

    whole = pl.BlockSpec(memory_space=pltpu.VMEM)
    held_in = [pltpu.with_memory_space_constraint(x, pltpu.VMEM) for x in (*tables, *hidden)]
    return pl.pallas_call(
        body,
        grid_spec=pltpu.PrefetchScalarGridSpec(
            num_scalar_prefetch=1,
            grid=(1,),
            in_specs=[whole] * (1 + len(held_in)),
            out_specs=whole,
            scratch_shapes=[
                pltpu.VMEM((lanes, width), BF16),
                pltpu.VMEM((count * rows, width), BF16),
            ],
        ),
        out_shape=jax.ShapeDtypeStruct((rank, lanes), F32),
        cost_estimate=cost(
            2 * lanes * count * rows * len(sources) * width,
            2 * (lanes + count * rows) * len(sources) * width,
            share,
        ),
        compiler_params=params(10),
        name="low_part",
    )(place, slots, *held_in)


def add_extra(place, low, slots, mine, other, keep, recv, first_row, pieces, per_shard, rank):
    _, planes, _, width = keep.shape
    rows, lanes = mine.shape[0], low.shape[1]
    half = planes // 2
    parts = {
        KEEP_Y: ((0,), range(planes)),
        SEND_Y: ((1,), range(planes)),
        KEEP_Z: ((0, 1), range(half)),
        SEND_Z: ((0, 1), range(half, planes)),
    }

    def body(place_ref, low_ref, slots_ref, m_ref, t_ref, k_ref, r_ref, *out_refs):
        rounded = low_ref[...].astype(BF16).astype(F32)
        wanted = slots_ref[...]
        spread = []
        for i in range(2):
            first = (place_ref[0] * PLANE + (place_ref[1] ^ i)) * per_shard
            masked = [jnp.where(wanted == first + a, rounded, 0.0) for a in range(per_shard)]
            spread.append(jnp.concatenate(masked, axis=0).T.astype(BF16))
        for (what, row, size), out_ref in zip(pieces, out_refs):
            start = row - first_row
            here = [value[start : start + size] for value in spread]
            rows_at = slice(row, row + size)
            for side_at, side in enumerate(parts[what][0]):
                for block_at, i in enumerate(parts[what][1]):
                    block = (place_ref[0] ^ halving(i, planes)) * PLANE + (place_ref[1] ^ (2 * side))
                    columns = pl.ds(pl.multiple_of(block * width, width), width)
                    own, other_own = m_ref[:, columns], t_ref[1, i, :, side * width : (side + 1) * width]
                    extra = jnp.dot(here[0], own, preferred_element_type=F32)
                    extra += jnp.dot(here[1], other_own, preferred_element_type=F32)
                    base = k_ref[side, i, rows_at] + r_ref[side, i, rows_at].astype(F32)
                    out_ref[side_at, block_at] = (base + extra).astype(out_ref.dtype)

    def shape(what, row, size):
        return (len(parts[what][0]), len(parts[what][1]), size, width)

    whole = pl.BlockSpec(memory_space=pltpu.VMEM)
    return pl.pallas_call(
        body,
        grid_spec=pltpu.PrefetchScalarGridSpec(
            num_scalar_prefetch=1,
            grid=(1,),
            in_specs=[whole] * 6,
            out_specs=[whole] * len(pieces),
        ),
        out_shape=[
            jax.ShapeDtypeStruct(shape(*piece), BF16 if piece[0] in (SEND_Y, SEND_Z) else F32)
            for piece in pieces
        ],
        cost_estimate=cost(4 * lanes * rows * planes * width, 10 * lanes * planes * width),
        compiler_params=params(10),
        name="add_extra",
    )(
        place,
        low,
        slots,
        *[pltpu.with_memory_space_constraint(x, pltpu.VMEM) for x in (mine, other, keep, recv)],
    )


def local(hidden, down_matrix, first_table, second_table, storage_index, request_adapter):
    steps, requests, units = hidden.shape
    per_shard, rank, all_units = first_table.shape
    features = second_table.shape[2]
    adapters = storage_index.shape[0]
    devices = all_units // units
    planes = devices // PLANE
    width = features // devices
    me = lax.axis_index("tensor").astype(jnp.int32)
    z, w = me // PLANE, me % PLANE
    place = jnp.stack([z, w, ((z == 1) | (z == 2)).astype(jnp.int32)])

    def in_plane(value, other):
        return lax.ppermute(value, "tensor", [(t, t ^ other) for t in range(devices)])

    def along(value, other):
        return lax.ppermute(value, "tensor", [(t, t ^ (other * PLANE)) for t in range(devices)])

    def hop(value, moves):
        pairs = [(a * PLANE + v, b * PLANE + v) for a, b in moves for v in range(PLANE)]
        return lax.ppermute(value, "tensor", pairs)

    table = jnp.arange(adapters, dtype=jnp.int32)
    slot_row = jnp.sum(
        jnp.where(request_adapter[:, None] == table[None, :], storage_index[None, :], 0), axis=1
    ).astype(jnp.int32)

    first = first_table.reshape(per_shard * rank, all_units)
    second = second_table.reshape(per_shard * rank, features)

    if planes == 4:
        order = jnp.stack([z, z ^ 1, jnp.where(z < 2, 2, 1), jnp.where(z < 2, 3, 0)])
    else:
        order = jnp.stack([z ^ o for o in range(planes)])
    split = planes // 2

    for_near = pack_factors(place, order, first, units, 2)
    near_y = in_plane(for_near, 2)
    hidden_z = hidden
    if planes == 4:
        near = along(hidden_z, 1)
        middle = hop(hidden_z, ((1, 2), (2, 1)))
    else:
        blocks = [hidden] + [along(hidden_z, o) for o in range(1, planes)]
        near = middle = blocks[1]
    for_far = pack_factors(place, order, after(first, for_near), units, 3)
    for_self = pack_factors(place, order, after(first, for_far), units, 0)
    for_core = pack_core(place, order, after(first, for_self), second, width)
    send, keep = base_blocks(place, after(hidden, for_core), down_matrix, planes, width)
    near, middle, send, near_y = lax.optimization_barrier((near, middle, send, near_y))
    from_core = in_plane(after(for_core, near), 1)
    far_y = in_plane(after(for_far, near_y), 3)
    recv = in_plane(send, 1)

    at_hand = [[hidden], [near]] if planes == 4 else [[block] for block in blocks[:split]]
    slots = jnp.tile(slot_row[None, :], (1, steps))

    def low_at(chunk, owners, tables, sources, first_plane):
        share = 1 if chunk[0] == 0 else 1000
        lanes = slots[:, chunk[0] * requests : chunk[1] * requests]
        return low_part(
            place, lanes, owners, tables, sources, first_plane, chunk, per_shard, rank, share
        )

    def early_of(*ready):
        near_by = (for_self, after(from_core, *ready), near_y)
        part = low_at((0, steps), (0, 1, 2), near_by, at_hand, 0)
        return part, low_at((0, steps), (3,), (after(far_y, part),), at_hand, 0)

    def late_of(chunk, plane, source, *ready):
        tables = (for_self, after(from_core, *ready), near_y, far_y)
        return low_at(chunk, range(PLANE), tables, [source], plane)

    if planes == 4:
        outward, across = ((1, 0), (2, 3)), ((1, 2), (2, 1))
        (a, b), (c, d) = LOW_CHUNKS
        outer_one = hop(middle[a:b], outward)
        middle_two = hop(near[a:b], across)
        outer_two = hop(after(middle_two, outer_one), outward)
        early, early_far = early_of(outer_one, middle_two)
        part = late_of((a, b), 2, [middle, outer_one], early_far)
        middle_two_first = middle_two
        middle_two = hop(after(near[c:d], middle_two), across)
        outer_one = hop(after(middle[c:d], outer_one), outward)
        last = late_of((a, b), 3, [middle_two_first, outer_two], part)
        outer_two = hop(after(middle_two, last), outward)
        late = [[part, last], [[middle, outer_one], [middle_two, outer_two]]]
        second_wave = [outer_one]
    else:
        early, early_far = early_of()
        late = [[[block] for block in blocks[split:]] for _ in LOW_CHUNKS]
        second_wave = []

    def core_sum(chunk, parts):
        low = (early + early_far)[:, chunk[0] * requests : chunk[1] * requests]
        for part in parts:
            low = low + part
        return low + in_plane(low, 1)

    flat = (2, planes, steps * requests, width)
    keep, recv = keep.reshape(flat), recv.reshape(flat)

    def with_extra(low, first_row, pieces):
        lanes = slots[:, : low.shape[1]]
        return add_extra(
            place, low, lanes, second, from_core, keep, recv, first_row, pieces, per_shard, rank
        )

    along_z = [1 << bit for bit in range(planes.bit_length() - 1)]
    y_first, z_first = ["y", *along_z], [*along_z[:1], "y", *along_z[1:]]
    plans = [list(plan) for plan in (y_first, z_first, y_first, z_first, y_first)]
    state = [None] * len(plans)

    def send(value, stage):
        return in_plane(value, 2) if stage == "y" else along(value, stage)

    def add(c, *ready):
        value, received = state[c]
        total = value + after(received, *ready).astype(F32)
        plans[c].pop(0)
        if not plans[c]:
            state[c] = (total, None)
            return total
        count = total.shape[0] // 2
        stays, goes = total[:count], total[count:].astype(BF16)
        if plans[c][0] == "y":
            stays, goes = stays[0], goes[0]
        state[c] = (stays, send(goes, plans[c][0]))
        return goes

    def begin(c, stays, goes):
        if plans[c][0] == "y":
            stays, goes = stays[0], goes[0]
        state[c] = (stays, send(goes, plans[c][0]))

    parts, ready = [], early_far
    for i, source in enumerate(late[0]):
        part = late_of(LOW_CHUNKS[0], split + i, source, ready) if isinstance(source, list) else source
        parts.append(part)
        ready = part
    low = core_sum(LOW_CHUNKS[0], parts)
    low = low + in_plane(low, 2)
    half = requests // 2
    rows = [0, requests + half // 2, 2 * requests, 3 * requests, 3 * requests + half, steps * requests]
    spans = [(a, b - a) for a, b in zip(rows, rows[1:])]
    (goes,) = with_extra(low, 0, [(SEND_Y, *spans[0])])
    low = after(low, goes, *second_wave)
    moved = send(goes[0], "y")
    stays, goes, next_stays = with_extra(
        low, 0, [(KEEP_Y, *spans[0]), (SEND_Z, *spans[1]), (KEEP_Z, *spans[1])]
    )
    state[0] = (stays[0], moved)
    parts, ready = [], (stays, goes, next_stays)
    for i, source in enumerate(late[1]):
        source = [after(array, *ready) for array in source]
        parts.append(late_of(LOW_CHUNKS[1], split + i, source, *ready))
        ready = (parts[-1],)
    begin(1, next_stays, after(goes, parts[0]))

    low = core_sum(LOW_CHUNKS[1], parts)
    across_y = in_plane(low, 2)
    done = add(0, low)
    low = low + after(across_y, done)
    (moved,) = with_extra(low, spans[2][0], [(SEND_Y, *spans[2])])
    done = add(1, moved)
    low = after(low, done)
    sent_y = send(moved[0], "y")
    stays, goes, next_stays, last_goes, last_stays = with_extra(
        low,
        spans[2][0],
        [
            (KEEP_Y, *spans[2]),
            (SEND_Z, *spans[3]),
            (KEEP_Z, *spans[3]),
            (SEND_Y, *spans[4]),
            (KEEP_Y, *spans[4]),
        ],
    )
    state[2] = (stays[0], sent_y)
    begin(3, next_stays, goes)
    begin(4, last_stays, last_goes)
    done = next_stays
    for c in (0, 2, 1, 3, 4, 2, 4, 3, 0, 1, 2, 4, 3):
        if plans[c]:
            done = add(c, done)
    for c in range(len(plans)):
        while plans[c]:
            done = add(c, done)
    outputs = [value[0].astype(BF16) for value, _ in state]
    return jnp.concatenate(outputs, axis=0).reshape(steps, requests, width)


def solution(mesh):
    in_specs = (
        P(None, "groups", "tensor"),
        P("tensor", None),
        P(("groups", "tensor"), None, None),
        P(("groups", "tensor"), None, None),
        P("groups"),
        P("groups"),
    )
    out_specs = P(None, "groups", "tensor")
    return jax.shard_map(local, mesh=mesh, in_specs=in_specs, out_specs=out_specs, check_vma=False)
```
